32 devices in a mesh: src: 4 (over y, core), tgt: 8 (over z, x).
Axes of the slice: x: 2, y: 2, z: 4, core: 2. Of those that a mesh axis runs over, the one named last changes fastest.
Arguments:
- sources: bfloat16 [64, 16384], P(None, ('src', 'tgt')), may hold values from -4 to 4
- targets: bfloat16 [64, 16384], P('src', 'tgt'), may hold values from -1 to 1
- potentials: float32 [16384], P('tgt'), may hold values from -2 to 11
- log_mass: float32 [16384], P('tgt'), may hold values from -3 to 0
Outputs:
- row_potentials: float32 [16384], P(('src', 'tgt'))
The draws below stay inside these ranges and needn't reach their ends.
All inputs are finite; a program needn't handle non-finite values.
Results may differ from the reference program's by a relative error of at most 0.0003.
Values may be sent and summed in bfloat16 or wider, within the bound.
No kernel may reach another device: no remote copies, remote signals or barrier semaphores. Data moves between devices by JAX's collectives and lax.ppermute only.
A program may use at most 64 MiB of HBM per device.

```python
import math
import jax
import jax.numpy as jnp
from jax import lax

LAT = 64
NS = 16384
NT = 16384


def base_points(key, normal_scale):
    first_key = jax.random.fold_in(key, 0)
    normals = jnp.clip(jax.random.normal(first_key, (LAT, NT), jnp.float32), -5.0, 5.0)
    return normal_scale * normals


def draw_targets(key, part):
    points = base_points(key, 0.125)
    return points.astype(jnp.bfloat16)


def draw_sources(key, part):
    key = jax.random.fold_in(key, 23)
    first_key = jax.random.fold_in(key, 0)
    points = 0.125 * jnp.clip(jax.random.normal(first_key, (LAT, NS), jnp.float32), -5.0, 5.0)
    return points.astype(jnp.bfloat16)


def draw_potentials(key, part):
    key = jax.random.fold_in(key, 37)
    level_key, noise_key = jax.random.split(key)
    level = jax.random.uniform(level_key, (), jnp.float32, 0.0, 4.0)
    noise = jnp.clip(jax.random.normal(noise_key, (NT,), jnp.float32), -5.0, 5.0)
    values = level + 0.03 * noise
    return values


def levels(stream_key, dims, cuts, smallest, top_value):
    loudness, own = 1.0, jax.random.fold_in(stream_key, 6)
    for position, shards_of in cuts:
        draws = jnp.exp(jax.random.uniform(jax.random.fold_in(own, position), (shards_of,), jnp.float32, smallest / len(cuts), top_value / len(cuts)))
        loudness = loudness * jnp.repeat(draws, dims[position] // shards_of).reshape([-1 if axis == position else 1 for axis in range(len(dims))])
    return loudness


def setup_inputs(seed: int = 0) -> dict:
    splits = jax.random.split(jax.random.key(seed), 5)
    return {
        "sources": draw_sources(jax.random.fold_in(splits[4], 71), 0),
        "targets": draw_targets(jax.random.fold_in(splits[4], 71), 0),
        "potentials": draw_potentials(jax.random.fold_in(splits[4], 71), 0),
        "log_mass": jnp.clip(-3.0 + 3.0 * jax.random.uniform(splits[3], (NT,), jnp.float32) ** levels(splits[3], (NT,), ((0, 8),), -0.2, 0.2), -3.0, 0.0),
    }


EPSILON = 0.05


def reference(sources, targets, potentials, log_mass):
    src_all = sources.astype(jnp.float32)
    tgt_all = targets.astype(jnp.float32)
    tgt_sq = jnp.sum(tgt_all * tgt_all, axis=0)
    src_sq = jnp.sum(src_all * src_all, axis=0)
    total_rows = src_all.shape[1]
    block_rows = math.gcd(total_rows, 256)

    def one_block(block_index):
        first = (block_index * block_rows).astype(jnp.int32)
        columns = lax.dynamic_slice_in_dim(src_all, first, block_rows, 1)
        norms = lax.dynamic_slice_in_dim(src_sq, first, block_rows, 0)
        crossed = jnp.dot(columns.T, tgt_all, precision=lax.Precision.HIGHEST)
        cost = 0.5 * (norms[:, None] + tgt_sq[None, :]) - crossed
        scores = (potentials[None, :] - cost) / EPSILON + log_mass[None, :]
        row_top = jnp.max(scores, axis=1)
        row_sum = jnp.sum(jnp.exp(scores - row_top[:, None]), axis=1)
        return -EPSILON * (row_top + jnp.log(row_sum))

    outputs = lax.map(one_block, jnp.arange(total_rows // block_rows, dtype=jnp.int32))
    return outputs.reshape(total_rows)
```

```python
import functools
import math

import jax
import jax.numpy as jnp
from jax import lax
from jax.experimental import pallas as pl
from jax.experimental.pallas import tpu as pltpu
from jax.sharding import PartitionSpec as P

EPSILON = 0.05
RATE = 1.0 / (EPSILON * math.log(2.0))
AXES = ("src", "tgt")
LANES = 128
CHUNK = 128
WIDE = 512


def flip(value, mask):
    n = lax.axis_size("src") * lax.axis_size("tgt")
    return lax.ppermute(value, AXES, [(i, i ^ mask) for i in range(n)])


def split3(value):
    first = value.astype(jnp.bfloat16).astype(jnp.float32)
    rest = value - first
    second = rest.astype(jnp.bfloat16).astype(jnp.float32)
    third = (rest - second).astype(jnp.bfloat16).astype(jnp.float32)
    return first, second, third


def pack_kernel(targets, potentials, log_mass, packed):
    rows, count = targets.shape
    packed[:, :count] = targets[...]
    bias = potentials[...] + EPSILON * log_mass[...]
    parts = split3(bias)
    deep = count // rows
    for k, part in enumerate(parts):
        packed[:, count + k * deep : count + (k + 1) * deep] = part.astype(jnp.bfloat16)


def pack_targets(targets, potentials, log_mass):
    rows, count = targets.shape
    deep = count // rows
    return pl.pallas_call(
        pack_kernel,
        out_shape=jax.ShapeDtypeStruct((rows, count + 3 * deep), jnp.bfloat16),
    )(targets, potentials.reshape(rows, deep), log_mass.reshape(rows, deep))


def score_kernel(src_bits, n_sources, *refs):
    src_refs, (tgt_own, tgt_far, bias_ref) = refs[:n_sources], refs[n_sources : n_sources + 3]
    out_ref, lhs, rhs = refs[n_sources + 3 :]
    count = tgt_own.shape[1]
    width = tgt_own.shape[0] + tgt_far.shape[0]

    step = min(1024, count)
    for start in range(0, count, step):
        cols = slice(start, start + step)
        points = jnp.concatenate([tgt_own[:, cols], tgt_far[:, cols]], axis=0)
        wide = points.astype(jnp.float32)
        half = 0.5 * jnp.sum(wide * wide, axis=0, keepdims=True)
        first, second, third = split3(bias_ref[:, cols] - half)
        place = lax.broadcasted_iota(jnp.int32, (LANES - width, step), 0)
        extra = jnp.where(place == 0, first, jnp.where(place == 1, second, jnp.where(place == 2, third, 0.0)))
        lhs[cols, :] = jnp.concatenate([points, extra.astype(jnp.bfloat16)], axis=0).T

    me = lax.axis_index("src")
    at = 0
    for ref in src_refs:
        points = ref[...].astype(jnp.float32)
        part = width >> src_bits
        blocks = [points[k * part : (k + 1) * part] for k in range(1 << src_bits)]
        for bit in range(src_bits):
            turned = ((me >> bit) & 1) == 1
            blocks = [jnp.where(turned, blocks[k ^ (1 << bit)], blocks[k]) for k in range(1 << src_bits)]
        points = jnp.concatenate(blocks[0::2] + blocks[1::2], axis=0)
        rhs[:width, at : at + ref.shape[1]] = points.astype(jnp.bfloat16)
        at += ref.shape[1]
    rhs[width:, :] = jnp.ones((LANES - width, at), jnp.bfloat16)

    def tile(index, carry):
        cols = pl.ds(pl.multiple_of(index * WIDE, WIDE), WIDE)
        block = rhs[:, cols]

        def product(j):
            found = jnp.dot(lhs[j * CHUNK : (j + 1) * CHUNK, :], block, preferred_element_type=jnp.float32)
            return found.reshape(CHUNK // 8, 8, WIDE)

        scores = product(0)
        top = jnp.max(scores, axis=0) * RATE
        total = jnp.sum(jnp.exp2(scores * RATE - top[None]), axis=0)
        for j in range(1, count // CHUNK):
            scores = product(j)
            higher = jnp.maximum(top, jnp.max(scores, axis=0) * RATE)
            total = total * jnp.exp2(top - higher) + jnp.sum(jnp.exp2(scores * RATE - higher[None]), axis=0)
            top = higher
        row_top = jnp.max(top, axis=0, keepdims=True)
        row_sum = jnp.sum(total * jnp.exp2(top - row_top), axis=0, keepdims=True)
        out_ref[:, cols] = row_top + jnp.log2(row_sum)
        return carry

    lax.fori_loop(0, at // WIDE, tile, 0)


def partial_logs(src_bits, sources, tgt_own, tgt_far, bias):
    count = tgt_own.shape[1]
    rows = sum(s.shape[1] for s in sources)
    return pl.pallas_call(
        functools.partial(score_kernel, src_bits, len(sources)),
        out_shape=jax.ShapeDtypeStruct((1, rows), jnp.float32),
        scratch_shapes=[
            pltpu.VMEM((count, LANES), jnp.bfloat16),
            pltpu.VMEM((LANES, rows), jnp.bfloat16),
        ],
        compiler_params=pltpu.CompilerParams(vmem_limit_bytes=48 << 20),
    )(*sources, tgt_own, tgt_far, bias)


def join(left, right):
    top = jnp.maximum(left, right)
    return top + jnp.log2(1.0 + jnp.exp2(-jnp.abs(left - right)))


def on_device(sources, targets, potentials, log_mass):
    n_src, n_tgt = lax.axis_size("src"), lax.axis_size("tgt")
    src_bits, tgt_bits = n_src.bit_length() - 1, n_tgt.bit_length() - 1
    shared = min(2, tgt_bits)
    count = targets.shape[1]
    owned = sources.shape[1]

    packed = pack_targets(targets, potentials, log_mass)
    held = [sources]
    for bit in range(shared):
        whole = held[0] if len(held) == 1 else jnp.concatenate(held, axis=1)
        held.append(flip(whole, 1 << bit))
    for bit in range(tgt_bits - 1, shared - 1, -1):
        packed = jnp.concatenate([packed, flip(packed, 1 << bit)], axis=1)

    pieces = packed.reshape(packed.shape[0], -1, packed.shape[1] >> (tgt_bits - shared))
    points = pieces[:, :, :count].reshape(targets.shape[0], -1)
    deep = count // targets.shape[0]
    parts = pieces[:, :, count:].astype(jnp.float32).reshape(targets.shape[0], -1, 3, deep)
    bias = (parts[:, :, 0] + parts[:, :, 1]) + parts[:, :, 2]
    bias = bias.transpose(1, 0, 2).reshape(1, -1)

    own = points
    for bit in range(1, src_bits):
        own = jnp.concatenate([own, flip(own, n_tgt << bit)], axis=0)
    far = flip(own, n_tgt)
    logs = partial_logs(src_bits, held, own, far, bias)[0]
    for bit in range(shared - 1, -1, -1):
        half = logs.shape[0] // 2
        logs = join(logs[:half], flip(logs[half:], 1 << bit))
    wide = sources.astype(jnp.float32)
    return 0.5 * jnp.sum(wide * wide, axis=0) - (1.0 / RATE) * logs


def solution(mesh):
    in_specs = (P(None, ("src", "tgt")), P("src", "tgt"), P("tgt"), P("tgt"))
    out_specs = P(("src", "tgt"))
    return jax.shard_map(
        on_device, mesh=mesh, in_specs=in_specs, out_specs=out_specs, check_vma=False
    )
```

```python
import functools
import math

import jax
import jax.numpy as jnp
from jax import lax
from jax.experimental import pallas as pl
from jax.experimental.pallas import tpu as pltpu
from jax.sharding import PartitionSpec as P

EPSILON = 0.05
RATE = 1.0 / (EPSILON * math.log(2.0))
AXES = ("src", "tgt")
LANES = 128
CHUNK = 128
WIDE = 512
VMEM = pl.BlockSpec(memory_space=pltpu.VMEM)
ANY = pl.BlockSpec(memory_space=pl.ANY)


def flip(value, mask):
    n = lax.axis_size("src") * lax.axis_size("tgt")
    return lax.ppermute(value, AXES, [(i, i ^ mask) for i in range(n)])


def split3(value):
    first = value.astype(jnp.bfloat16).astype(jnp.float32)
    rest = value - first
    second = rest.astype(jnp.bfloat16).astype(jnp.float32)
    third = (rest - second).astype(jnp.bfloat16).astype(jnp.float32)
    return first, second, third


def pack_kernel(targets, potentials, log_mass, packed, potentials_here, log_mass_here, sems):
    rows, count = targets.shape
    copies = [
        pltpu.make_async_copy(potentials, potentials_here, sems.at[0]),
        pltpu.make_async_copy(log_mass, log_mass_here, sems.at[1]),
        pltpu.make_async_copy(targets, packed.at[:, pl.ds(0, count)], sems.at[2]),
    ]
    for copy in copies:
        copy.start()
    copies[0].wait()
    copies[1].wait()
    bias = potentials_here[...] + EPSILON * log_mass_here[...]
    deep = count // rows
    for k, part in enumerate(split3(bias)):
        packed[:, count + k * deep : count + (k + 1) * deep] = part.astype(jnp.bfloat16)
    copies[2].wait()


def pack_targets(targets, potentials, log_mass):
    rows, count = targets.shape
    deep = count // rows
    return pl.pallas_call(
        pack_kernel,
        out_shape=jax.ShapeDtypeStruct((rows, count + 3 * deep), jnp.bfloat16),
        in_specs=[ANY] * 3,
        out_specs=VMEM,
        scratch_shapes=[
            pltpu.VMEM((rows, deep), jnp.float32),
            pltpu.VMEM((rows, deep), jnp.float32),
            pltpu.SemaphoreType.DMA((3,)),
        ],
    )(targets, potentials.reshape(rows, deep), log_mass.reshape(rows, deep))


def place_targets(tgt_own, tgt_far, bias_ref, lhs):
    count = tgt_own.shape[1]
    width = tgt_own.shape[0] + tgt_far.shape[0]
    step = min(1024, count)
    for start in range(0, count, step):
        cols = slice(start, start + step)
        points = jnp.concatenate([tgt_own[:, cols], tgt_far[:, cols]], axis=0)
        wide = points.astype(jnp.float32)
        half = 0.5 * jnp.sum(wide * wide, axis=0, keepdims=True)
        first, second, third = split3(bias_ref[:, cols] - half)
        place = lax.broadcasted_iota(jnp.int32, (LANES - width, step), 0)
        extra = jnp.where(place < 6, 1.0, 0.0)
        for k, part in enumerate((first, second, third)):
            extra = jnp.where(place == k, part, extra)
        lhs[cols, :] = jnp.concatenate([points, extra.astype(jnp.bfloat16)], axis=0).T


def place_sources(src_bits, src_ref, rhs):
    width, rows = src_ref.shape
    points = src_ref[...].astype(jnp.float32)
    me = lax.axis_index("src")
    part = width >> src_bits
    blocks = [points[k * part : (k + 1) * part] for k in range(1 << src_bits)]
    for bit in range(src_bits):
        turned = ((me >> bit) & 1) == 1
        blocks = [jnp.where(turned, blocks[k ^ (1 << bit)], blocks[k]) for k in range(1 << src_bits)]
    points = jnp.concatenate(blocks[0::2] + blocks[1::2], axis=0)
    rhs[:width, :] = points.astype(jnp.bfloat16)
    place = lax.broadcasted_iota(jnp.int32, (LANES - width, rows), 0)
    rhs[width:, :] = jnp.where(place < 3, 1.0, 0.0).astype(jnp.bfloat16)


def log_sums(width, lhs, rhs, out_ref):
    count, rows = lhs.shape[0], rhs.shape[1]

    def product(j, block):
        chunk = pl.ds(pl.multiple_of(j * CHUNK, CHUNK), CHUNK)
        found = jnp.dot(lhs[chunk, :], block, preferred_element_type=jnp.float32)
        return found.reshape(CHUNK // 8, 8, found.shape[1])

    place = lax.broadcasted_iota(jnp.int32, (LANES - width, WIDE), 0)
    for start in range(0, rows, WIDE):
        cols = slice(start, start + WIDE)
        high = jnp.max(jnp.max(product(0, rhs[:, cols]), axis=0), axis=0, keepdims=True)
        extra = jnp.where(place < 3, 1.0, 0.0)
        for k, part in enumerate(split3(-high)):
            extra = jnp.where(place == 3 + k, part, extra)
        rhs[width:, cols] = extra.astype(jnp.bfloat16)
        out_ref[:, cols] = high * RATE
    worst = jnp.zeros((1, WIDE), jnp.float32)
    for start in range(0, rows, WIDE):
        cols = slice(start, start + WIDE)
        block = rhs[:, cols]
        total = jnp.zeros((8, WIDE), jnp.float32)
        for j in range(count // CHUNK):
            total = total + jnp.sum(jnp.exp2(product(j, block) * RATE), axis=0)
        row_sum = jnp.sum(total, axis=0, keepdims=True)
        out_ref[:, cols] += jnp.log2(row_sum)
        worst = jnp.maximum(worst, row_sum)

    @pl.when(jnp.logical_not(jnp.max(worst) < jnp.inf))
    def _():
        for start in range(0, rows, WIDE):
            cols = slice(start, start + WIDE)
            extra = jnp.where(place < 3, 1.0, 0.0)
            rhs[width:, cols] = extra.astype(jnp.bfloat16)
            block = rhs[:, cols]

            def step(j, carry):
                top, total = carry
                scores = product(j, block) * RATE
                higher = jnp.maximum(top, jnp.max(scores, axis=0))
                total = total * jnp.exp2(top - higher) + jnp.sum(jnp.exp2(scores - higher[None]), axis=0)
                return higher, total

            first = jnp.max(product(0, block) * RATE, axis=0)
            top, total = lax.fori_loop(0, count // CHUNK, step, (first, jnp.zeros_like(first)))
            row_top = jnp.max(top, axis=0, keepdims=True)
            row_sum = jnp.sum(total * jnp.exp2(top - row_top), axis=0, keepdims=True)
            out_ref[:, cols] = row_top + jnp.log2(row_sum)


def first_kernel(src_bits, src_ref, tgt_own, tgt_far, bias_ref, out_ref, lhs, rhs):
    place_targets(tgt_own, tgt_far, bias_ref, lhs)
    place_sources(src_bits, src_ref, rhs)
    log_sums(src_ref.shape[0], lhs, rhs, out_ref)


def next_kernel(src_bits, src_ref, lhs, out_ref, rhs):
    place_sources(src_bits, src_ref, rhs)
    log_sums(src_ref.shape[0], lhs, rhs, out_ref)


def estimate(rows, count):
    return pl.CostEstimate(flops=2 * rows * count * LANES, bytes_accessed=2 * count * LANES, transcendentals=rows * count)


def first_logs(src_bits, sources, tgt_own, tgt_far, bias):
    count, rows = tgt_own.shape[1], sources.shape[1]
    return pl.pallas_call(
        functools.partial(first_kernel, src_bits),
        out_shape=(
            jax.ShapeDtypeStruct((1, rows), jnp.float32),
            jax.ShapeDtypeStruct((count, LANES), jnp.bfloat16),
        ),
        in_specs=[VMEM] * 4,
        out_specs=(VMEM, VMEM),
        scratch_shapes=[pltpu.VMEM((LANES, rows), jnp.bfloat16)],
        cost_estimate=estimate(rows, count),
        compiler_params=pltpu.CompilerParams(vmem_limit_bytes=48 << 20),
    )(sources, tgt_own, tgt_far, bias)


def next_logs(src_bits, sources, lhs):
    count, rows = lhs.shape[0], sources.shape[1]
    return pl.pallas_call(
        functools.partial(next_kernel, src_bits),
        out_shape=jax.ShapeDtypeStruct((1, rows), jnp.float32),
        in_specs=[VMEM] * 2,
        out_specs=VMEM,
        scratch_shapes=[pltpu.VMEM((LANES, rows), jnp.bfloat16)],
        cost_estimate=estimate(rows, count),
        compiler_params=pltpu.CompilerParams(vmem_limit_bytes=48 << 20),
    )(sources, lhs)


def join(left, right):
    top = jnp.maximum(left, right)
    return top + jnp.log2(1.0 + jnp.exp2(-jnp.abs(left - right)))


def on_device(sources, targets, potentials, log_mass):
    n_src, n_tgt = lax.axis_size("src"), lax.axis_size("tgt")
    src_bits, tgt_bits = n_src.bit_length() - 1, n_tgt.bit_length() - 1
    shared = min(2, tgt_bits)
    masks = [(1 << bit) | n_tgt for bit in range(shared)]
    count = targets.shape[1]

    packed = pack_targets(targets, potentials, log_mass)
    own_sources, packed = lax.optimization_barrier((sources, packed))
    for bit in range(tgt_bits - 1, shared - 1, -1):
        packed = jnp.concatenate([packed, flip(packed, 1 << bit)], axis=1)
    held = [own_sources]
    for mask in masks:
        whole = held[0] if len(held) == 1 else jnp.concatenate(held, axis=1)
        held.append(flip(whole, mask))

    pieces = packed.reshape(packed.shape[0], -1, packed.shape[1] >> (tgt_bits - shared))
    points = pieces[:, :, :count].reshape(targets.shape[0], -1)
    deep = count // targets.shape[0]
    parts = pieces[:, :, count:].astype(jnp.float32).reshape(targets.shape[0], -1, 3, deep)
    bias = (parts[:, :, 0] + parts[:, :, 1]) + parts[:, :, 2]
    bias = bias.transpose(1, 0, 2).reshape(1, -1)

    own = points
    for bit in range(1, src_bits):
        own = jnp.concatenate([own, flip(own, n_tgt << bit)], axis=0)
    far = flip(own, n_tgt)

    owned = sources.shape[1]
    arrived = []
    logs, lhs = first_logs(src_bits, held[-1], own, far, bias)
    for k in range(shared, 0, -1):
        for other in arrived:
            logs = join(logs, other[:, owned << (k - 1) : owned << k])
        arrived.append(flip(logs, masks[k - 1]))
        logs = next_logs(src_bits, held[k - 1], lhs)
    for other in arrived:
        logs = join(logs, other[:, :owned])
    wide = sources.astype(jnp.float32)
    return 0.5 * jnp.sum(wide * wide, axis=0) - (1.0 / RATE) * logs[0]


def solution(mesh):
    in_specs = (P(None, ("src", "tgt")), P("src", "tgt"), P("tgt"), P("tgt"))
    out_specs = P(("src", "tgt"))
    return jax.shard_map(
        on_device, mesh=mesh, in_specs=in_specs, out_specs=out_specs, check_vma=False
    )
```

```python
import functools
import math

import jax
import jax.numpy as jnp
from jax import lax
from jax.experimental import pallas as pl
from jax.experimental.pallas import tpu as pltpu
from jax.sharding import PartitionSpec as P

EPSILON = 0.05
RATE = 1.0 / (EPSILON * math.log(2.0))
AXES = ("src", "tgt")
LANES = 128
CHUNK = 128
WIDE = 512
VMEM = pl.BlockSpec(memory_space=pltpu.VMEM)
ANY = pl.BlockSpec(memory_space=pl.ANY)


def flip(value, mask):
    n = lax.axis_size("src") * lax.axis_size("tgt")
    return lax.ppermute(value, AXES, [(i, i ^ mask) for i in range(n)])


def split3(value):
    first = value.astype(jnp.bfloat16).astype(jnp.float32)
    rest = value - first
    second = rest.astype(jnp.bfloat16).astype(jnp.float32)
    third = (rest - second).astype(jnp.bfloat16).astype(jnp.float32)
    return first, second, third


def load_kernel(targets, potentials, log_mass, targets_here, bias, scratch, sems):
    copies = [
        pltpu.make_async_copy(potentials, scratch.at[0], sems.at[0]),
        pltpu.make_async_copy(log_mass, scratch.at[1], sems.at[1]),
        pltpu.make_async_copy(targets, targets_here, sems.at[2]),
    ]
    for copy in copies:
        copy.start()
    copies[0].wait()
    copies[1].wait()
    bias[...] = scratch[0] + EPSILON * scratch[1]
    copies[2].wait()


def load(targets, potentials, log_mass):
    rows = potentials.shape[0] // LANES
    return pl.pallas_call(
        load_kernel,
        out_shape=(pltpu.VMEM(targets.shape, targets.dtype), pltpu.VMEM((rows, LANES), jnp.float32)),
        in_specs=[ANY] * 3,
        out_specs=(VMEM,) * 2,
        scratch_shapes=[pltpu.VMEM((2, rows, LANES), jnp.float32), pltpu.SemaphoreType.DMA((3,))],
        compiler_params=pltpu.CompilerParams(vmem_limit_bytes=8 << 20),
    )(targets, potentials.reshape(rows, LANES), log_mass.reshape(rows, LANES))


def place_targets(tgt_own, tgt_far, bias_ref, lhs):
    count = tgt_own.shape[1]
    width = tgt_own.shape[0] + tgt_far.shape[0]
    step = min(1024, count)
    for start in range(0, count, step):
        cols = slice(start, start + step)
        points = jnp.concatenate([tgt_own[:, cols], tgt_far[:, cols]], axis=0)
        wide = points.astype(jnp.float32)
        half = 0.5 * jnp.sum(wide * wide, axis=0, keepdims=True)
        first, second, third = split3(bias_ref[:, cols] - half)
        place = lax.broadcasted_iota(jnp.int32, (LANES - width, step), 0)
        extra = jnp.where(place < 6, 1.0, 0.0)
        for k, part in enumerate((first, second, third)):
            extra = jnp.where(place == k, part, extra)
        lhs[cols, :] = jnp.concatenate([points, extra.astype(jnp.bfloat16)], axis=0).T


def place_sources(src_bits, src_ref, rhs):
    width, rows = src_ref.shape
    points = src_ref[...].astype(jnp.float32)
    me = lax.axis_index("src")
    part = width >> src_bits
    blocks = [points[k * part : (k + 1) * part] for k in range(1 << src_bits)]
    for bit in range(src_bits):
        turned = ((me >> bit) & 1) == 1
        blocks = [jnp.where(turned, blocks[k ^ (1 << bit)], blocks[k]) for k in range(1 << src_bits)]
    points = jnp.concatenate(blocks[0::2] + blocks[1::2], axis=0)
    rhs[:width, :] = points.astype(jnp.bfloat16)
    place = lax.broadcasted_iota(jnp.int32, (LANES - width, rows), 0)
    rhs[width:, :] = jnp.where(place < 3, 1.0, 0.0).astype(jnp.bfloat16)


def sources_kernel(src_bits, *refs):
    count = len(refs) // 2
    for src_ref, rhs in zip(refs[:count], refs[count:], strict=True):
        place_sources(src_bits, src_ref, rhs)


def placed_sources(src_bits, held):
    return pl.pallas_call(
        functools.partial(sources_kernel, src_bits),
        out_shape=tuple(pltpu.VMEM((LANES, piece.shape[1]), jnp.bfloat16) for piece in held),
        in_specs=[VMEM] * len(held),
        out_specs=(VMEM,) * len(held),
        cost_estimate=pl.CostEstimate(flops=4 << 30, bytes_accessed=0, transcendentals=0),
        compiler_params=pltpu.CompilerParams(vmem_limit_bytes=8 << 20),
    )(*held)


def log_sums(width, lhs, rhs, out_ref):
    count, rows = lhs.shape[0], rhs.shape[1]

    def product(j, block):
        chunk = pl.ds(pl.multiple_of(j * CHUNK, CHUNK), CHUNK)
        found = jnp.dot(lhs[chunk, :], block, preferred_element_type=jnp.float32)
        return found.reshape(CHUNK // 8, 8, found.shape[1])

    place = lax.broadcasted_iota(jnp.int32, (LANES - width, WIDE), 0)
    for start in range(0, rows, WIDE):
        cols = slice(start, start + WIDE)
        high = jnp.max(jnp.max(product(0, rhs[:, cols]), axis=0), axis=0, keepdims=True)
        extra = jnp.where(place < 3, 1.0, 0.0)
        for k, part in enumerate(split3(-high)):
            extra = jnp.where(place == 3 + k, part, extra)
        rhs[width:, cols] = extra.astype(jnp.bfloat16)
        out_ref[:, cols] = high * RATE
    worst = jnp.zeros((1, WIDE), jnp.float32)
    for start in range(0, rows, WIDE):
        cols = slice(start, start + WIDE)
        block = rhs[:, cols]
        total = jnp.zeros((8, WIDE), jnp.float32)
        for j in range(count // CHUNK):
            total = total + jnp.sum(jnp.exp2(product(j, block) * RATE), axis=0)
        row_sum = jnp.sum(total, axis=0, keepdims=True)
        out_ref[:, cols] += jnp.log2(row_sum)
        worst = jnp.maximum(worst, row_sum)

    @pl.when(jnp.logical_not(jnp.max(worst) < jnp.inf))
    def _():
        for start in range(0, rows, WIDE):
            cols = slice(start, start + WIDE)
            extra = jnp.where(place < 3, 1.0, 0.0)
            rhs[width:, cols] = extra.astype(jnp.bfloat16)
            block = rhs[:, cols]

            def step(j, carry):
                top, total = carry
                scores = product(j, block) * RATE
                higher = jnp.maximum(top, jnp.max(scores, axis=0))
                total = total * jnp.exp2(top - higher) + jnp.sum(jnp.exp2(scores - higher[None]), axis=0)
                return higher, total

            first = jnp.max(product(0, block) * RATE, axis=0)
            top, total = lax.fori_loop(0, count // CHUNK, step, (first, jnp.zeros_like(first)))
            row_top = jnp.max(top, axis=0, keepdims=True)
            row_sum = jnp.sum(total * jnp.exp2(top - row_top), axis=0, keepdims=True)
            out_ref[:, cols] = row_top + jnp.log2(row_sum)


def first_kernel(placed, tgt_own, tgt_far, bias_ref, out_ref, lhs, rhs):
    place_targets(tgt_own, tgt_far, bias_ref, lhs)
    rhs[...] = placed[...]
    log_sums(tgt_own.shape[0] + tgt_far.shape[0], lhs, rhs, out_ref)


def next_kernel(width, placed, lhs, out_ref, rhs):
    rhs[...] = placed[...]
    log_sums(width, lhs, rhs, out_ref)


def estimate(rows, count):
    return pl.CostEstimate(flops=2 * rows * count * LANES, bytes_accessed=2 * count * LANES, transcendentals=rows * count)


def first_logs(placed, tgt_own, tgt_far, bias):
    count, rows = tgt_own.shape[1], placed.shape[1]
    return pl.pallas_call(
        first_kernel,
        out_shape=(pltpu.VMEM((1, rows), jnp.float32), pltpu.VMEM((count, LANES), jnp.bfloat16)),
        in_specs=[VMEM] * 4,
        out_specs=(VMEM, VMEM),
        scratch_shapes=[pltpu.VMEM((LANES, rows), jnp.bfloat16)],
        cost_estimate=estimate(rows, count),
        compiler_params=pltpu.CompilerParams(vmem_limit_bytes=48 << 20),
    )(placed, tgt_own, tgt_far, bias)


def next_logs(width, placed, lhs):
    count, rows = lhs.shape[0], placed.shape[1]
    return pl.pallas_call(
        functools.partial(next_kernel, width),
        out_shape=pltpu.VMEM((1, rows), jnp.float32),
        in_specs=[VMEM] * 2,
        out_specs=VMEM,
        scratch_shapes=[pltpu.VMEM((LANES, rows), jnp.bfloat16)],
        cost_estimate=estimate(rows, count),
        compiler_params=pltpu.CompilerParams(vmem_limit_bytes=48 << 20),
    )(placed, lhs)


def join(left, right):
    top = jnp.maximum(left, right)
    return top + jnp.log2(1.0 + jnp.exp2(-jnp.abs(left - right)))


def gather(value, masks, axis):
    for mask in masks:
        value = jnp.concatenate([value, flip(value, mask)], axis=axis)
    return value


def on_device(sources, targets, potentials, log_mass):
    n_src, n_tgt = lax.axis_size("src"), lax.axis_size("tgt")
    src_bits, tgt_bits = n_src.bit_length() - 1, n_tgt.bit_length() - 1
    shared = min(2, tgt_bits)
    masks = [(1 << bit) | n_tgt for bit in range(shared)]
    col_masks = [1 << bit for bit in range(tgt_bits - 1, shared - 1, -1)]
    row_masks = [n_tgt << bit for bit in range(1, src_bits)]

    targets_here, bias = load(targets, potentials, log_mass)
    held = [sources]
    for mask in masks:
        whole = held[0] if len(held) == 1 else jnp.concatenate(held, axis=1)
        held.append(flip(whole, mask))
    if len(col_masks) == 1 and len(row_masks) == 1:
        beside = flip(targets, col_masks[0])
        beside, bias = lax.optimization_barrier((beside, bias))
        below = flip(targets, row_masks[0])
        corner = flip(beside, row_masks[0])
        upper = jnp.concatenate([targets_here, beside], axis=1)
        lower = jnp.concatenate([below, corner], axis=1)
        own = jnp.concatenate([upper, lower], axis=0)
    else:
        own = gather(gather(targets_here, col_masks, 1), row_masks, 0)
    bias = gather(bias, col_masks, 0).reshape(1, -1)
    far = flip(own, n_tgt)
    placed = placed_sources(src_bits, held)

    owned = sources.shape[1]
    arrived = []
    logs, lhs = first_logs(placed[-1], own, far, bias)
    for k in range(shared, 0, -1):
        for other in arrived:
            logs = join(logs, other[:, owned << (k - 1) : owned << k])
        arrived.append(flip(logs, masks[k - 1]))
        logs = next_logs(sources.shape[0], placed[k - 1], lhs)
    for other in arrived:
        logs = join(logs, other[:, :owned])
    wide = sources.astype(jnp.float32)
    return 0.5 * jnp.sum(wide * wide, axis=0) - (1.0 / RATE) * logs[0]


def solution(mesh):
    in_specs = (P(None, ("src", "tgt")), P("src", "tgt"), P("tgt"), P("tgt"))
    out_specs = P(("src", "tgt"))
    return jax.shard_map(
        on_device, mesh=mesh, in_specs=in_specs, out_specs=out_specs, check_vma=False
    )
```

```python
import functools
import math

import jax
import jax.numpy as jnp
from jax import lax
from jax.experimental import pallas as pl
from jax.experimental.pallas import tpu as pltpu
from jax.sharding import PartitionSpec as P

EPSILON = 0.05
RATE = 1.0 / (EPSILON * math.log(2.0))
AXES = ("src", "tgt")
LANES = 128
CHUNK = 128
WIDE = 512
VMEM = pl.BlockSpec(memory_space=pltpu.VMEM)
ANY = pl.BlockSpec(memory_space=pl.ANY)


def flip(value, mask):
    n = lax.axis_size("src") * lax.axis_size("tgt")
    return lax.ppermute(value, AXES, [(i, i ^ mask) for i in range(n)])


def split3(value):
    first = value.astype(jnp.bfloat16).astype(jnp.float32)
    rest = value - first
    second = rest.astype(jnp.bfloat16).astype(jnp.float32)
    third = (rest - second).astype(jnp.bfloat16).astype(jnp.float32)
    return first, second, third


def load_kernel(targets, potentials, log_mass, targets_here, bias, parts, scratch, sems):
    copies = [
        pltpu.make_async_copy(potentials, scratch.at[0], sems.at[0]),
        pltpu.make_async_copy(log_mass, scratch.at[1], sems.at[1]),
        pltpu.make_async_copy(targets, targets_here, sems.at[2]),
    ]
    for copy in copies:
        copy.start()
    copies[0].wait()
    copies[1].wait()
    bias[...] = scratch[0] + EPSILON * scratch[1]
    deep = bias.shape[1]
    for k, part in enumerate(split3(bias[...])):
        parts[:, k * deep : (k + 1) * deep] = part.astype(jnp.bfloat16)
    copies[2].wait()


def load(targets, potentials, log_mass):
    rows, count = targets.shape
    deep = count // rows
    return pl.pallas_call(
        load_kernel,
        out_shape=(
            pltpu.VMEM((rows, count), targets.dtype),
            pltpu.VMEM((rows, deep), jnp.float32),
            pltpu.VMEM((rows, 3 * deep), jnp.bfloat16),
        ),
        in_specs=[ANY] * 3,
        out_specs=(VMEM,) * 3,
        scratch_shapes=[pltpu.VMEM((2, rows, deep), jnp.float32), pltpu.SemaphoreType.DMA((3,))],
    )(targets, potentials.reshape(rows, deep), log_mass.reshape(rows, deep))


def place_targets(tgt_own, tgt_far, bias_ref, lhs):
    count = tgt_own.shape[1]
    width = tgt_own.shape[0] + tgt_far.shape[0]
    step = min(1024, count)
    for start in range(0, count, step):
        cols = slice(start, start + step)
        points = jnp.concatenate([tgt_own[:, cols], tgt_far[:, cols]], axis=0)
        wide = points.astype(jnp.float32)
        half = 0.5 * jnp.sum(wide * wide, axis=0, keepdims=True)
        first, second, third = split3(bias_ref[:, cols] - half)
        place = lax.broadcasted_iota(jnp.int32, (LANES - width, step), 0)
        extra = jnp.where(place < 6, 1.0, 0.0)
        for k, part in enumerate((first, second, third)):
            extra = jnp.where(place == k, part, extra)
        lhs[cols, :] = jnp.concatenate([points, extra.astype(jnp.bfloat16)], axis=0).T


def place_sources(src_bits, src_ref, rhs):
    width, rows = src_ref.shape
    points = src_ref[...].astype(jnp.float32)
    me = lax.axis_index("src")
    part = width >> src_bits
    blocks = [points[k * part : (k + 1) * part] for k in range(1 << src_bits)]
    for bit in range(src_bits):
        turned = ((me >> bit) & 1) == 1
        blocks = [jnp.where(turned, blocks[k ^ (1 << bit)], blocks[k]) for k in range(1 << src_bits)]
    points = jnp.concatenate(blocks[0::2] + blocks[1::2], axis=0)
    rhs[:width, :] = points.astype(jnp.bfloat16)
    place = lax.broadcasted_iota(jnp.int32, (LANES - width, rows), 0)
    rhs[width:, :] = jnp.where(place < 3, 1.0, 0.0).astype(jnp.bfloat16)


def sources_kernel(src_bits, *refs):
    count = len(refs) // 2
    for src_ref, rhs in zip(refs[:count], refs[count:], strict=True):
        place_sources(src_bits, src_ref, rhs)


def placed_sources(src_bits, held):
    return pl.pallas_call(
        functools.partial(sources_kernel, src_bits),
        out_shape=tuple(pltpu.VMEM((LANES, piece.shape[1]), jnp.bfloat16) for piece in held),
        in_specs=[VMEM] * len(held),
        out_specs=(VMEM,) * len(held),
        cost_estimate=pl.CostEstimate(flops=4 << 30, bytes_accessed=0, transcendentals=0),
        compiler_params=pltpu.CompilerParams(vmem_limit_bytes=8 << 20),
    )(*held)


def log_sums(width, lhs, rhs, out_ref):
    count, rows = lhs.shape[0], rhs.shape[1]

    def product(j, block):
        chunk = pl.ds(pl.multiple_of(j * CHUNK, CHUNK), CHUNK)
        found = jnp.dot(lhs[chunk, :], block, preferred_element_type=jnp.float32)
        return found.reshape(CHUNK // 8, 8, found.shape[1])

    place = lax.broadcasted_iota(jnp.int32, (LANES - width, WIDE), 0)
    for start in range(0, rows, WIDE):
        cols = slice(start, start + WIDE)
        high = jnp.max(jnp.max(product(0, rhs[:, cols]), axis=0), axis=0, keepdims=True)
        extra = jnp.where(place < 3, 1.0, 0.0)
        for k, part in enumerate(split3(-high)):
            extra = jnp.where(place == 3 + k, part, extra)
        rhs[width:, cols] = extra.astype(jnp.bfloat16)
        out_ref[:, cols] = high * RATE
    worst = jnp.zeros((1, WIDE), jnp.float32)
    for start in range(0, rows, WIDE):
        cols = slice(start, start + WIDE)
        block = rhs[:, cols]
        total = jnp.zeros((8, WIDE), jnp.float32)
        for j in range(count // CHUNK):
            total = total + jnp.sum(jnp.exp2(product(j, block) * RATE), axis=0)
        row_sum = jnp.sum(total, axis=0, keepdims=True)
        out_ref[:, cols] += jnp.log2(row_sum)
        worst = jnp.maximum(worst, row_sum)

    @pl.when(jnp.logical_not(jnp.max(worst) < jnp.inf))
    def _():
        for start in range(0, rows, WIDE):
            cols = slice(start, start + WIDE)
            extra = jnp.where(place < 3, 1.0, 0.0)
            rhs[width:, cols] = extra.astype(jnp.bfloat16)
            block = rhs[:, cols]

            def step(j, carry):
                top, total = carry
                scores = product(j, block) * RATE
                higher = jnp.maximum(top, jnp.max(scores, axis=0))
                total = total * jnp.exp2(top - higher) + jnp.sum(jnp.exp2(scores - higher[None]), axis=0)
                return higher, total

            first = jnp.max(product(0, block) * RATE, axis=0)
            top, total = lax.fori_loop(0, count // CHUNK, step, (first, jnp.zeros_like(first)))
            row_top = jnp.max(top, axis=0, keepdims=True)
            row_sum = jnp.sum(total * jnp.exp2(top - row_top), axis=0, keepdims=True)
            out_ref[:, cols] = row_top + jnp.log2(row_sum)


def first_kernel(placed, tgt_own, tgt_far, bias_ref, out_ref, lhs, rhs):
    place_targets(tgt_own, tgt_far, bias_ref, lhs)
    rhs[...] = placed[...]
    log_sums(tgt_own.shape[0] + tgt_far.shape[0], lhs, rhs, out_ref)


def next_kernel(width, placed, lhs, out_ref, rhs):
    rhs[...] = placed[...]
    log_sums(width, lhs, rhs, out_ref)


def estimate(rows, count):
    return pl.CostEstimate(flops=2 * rows * count * LANES, bytes_accessed=2 * count * LANES, transcendentals=rows * count)


def first_logs(placed, tgt_own, tgt_far, bias):
    count, rows = tgt_own.shape[1], placed.shape[1]
    return pl.pallas_call(
        first_kernel,
        out_shape=(pltpu.VMEM((1, rows), jnp.float32), pltpu.VMEM((count, LANES), jnp.bfloat16)),
        in_specs=[VMEM] * 4,
        out_specs=(VMEM, VMEM),
        scratch_shapes=[pltpu.VMEM((LANES, rows), jnp.bfloat16)],
        cost_estimate=estimate(rows, count),
        compiler_params=pltpu.CompilerParams(vmem_limit_bytes=48 << 20),
    )(placed, tgt_own, tgt_far, bias)


def next_logs(width, placed, lhs):
    count, rows = lhs.shape[0], placed.shape[1]
    return pl.pallas_call(
        functools.partial(next_kernel, width),
        out_shape=pltpu.VMEM((1, rows), jnp.float32),
        in_specs=[VMEM] * 2,
        out_specs=VMEM,
        scratch_shapes=[pltpu.VMEM((LANES, rows), jnp.bfloat16)],
        cost_estimate=estimate(rows, count),
        compiler_params=pltpu.CompilerParams(vmem_limit_bytes=48 << 20),
    )(placed, lhs)


def join(left, right):
    top = jnp.maximum(left, right)
    return top + jnp.log2(1.0 + jnp.exp2(-jnp.abs(left - right)))


def gather(value, masks, axis):
    for mask in masks:
        value = jnp.concatenate([value, flip(value, mask)], axis=axis)
    return value


def on_device(sources, targets, potentials, log_mass):
    n_src, n_tgt = lax.axis_size("src"), lax.axis_size("tgt")
    src_bits, tgt_bits = n_src.bit_length() - 1, n_tgt.bit_length() - 1
    shared = min(2, tgt_bits)
    masks = [(1 << bit) | n_tgt for bit in range(shared - 1, -1, -1)]
    col_masks = [1 << bit for bit in range(tgt_bits - 1, shared - 1, -1)]
    row_masks = [n_tgt << bit for bit in range(1, src_bits)]

    targets_here, bias, parts = load(targets, potentials, log_mass)
    held = [sources]
    for mask in masks:
        whole = held[0] if len(held) == 1 else jnp.concatenate(held, axis=1)
        held.append(flip(whole, mask))
    if len(col_masks) == 1 and len(row_masks) == 1:
        count, deep = targets.shape[1], bias.shape[1]
        beside = flip(targets, col_masks[0])
        below = flip(targets, row_masks[0])
        corner = flip(jnp.concatenate([below, parts], axis=1), col_masks[0])
        parts = corner[:, count:].astype(jnp.float32)
        there = (parts[:, :deep] + parts[:, deep : 2 * deep]) + parts[:, 2 * deep :]
        bias = jnp.concatenate([bias, there], axis=0)
        upper = jnp.concatenate([targets_here, beside], axis=1)
        lower = jnp.concatenate([below, corner[:, :count]], axis=1)
        own = jnp.concatenate([upper, lower], axis=0)
    else:
        own = gather(gather(targets_here, col_masks, 1), row_masks, 0)
        bias = gather(bias, col_masks, 0)
    bias = bias.reshape(1, -1)
    far = flip(own, n_tgt)
    placed = placed_sources(src_bits, held)

    owned = sources.shape[1]
    arrived = []
    logs, lhs = first_logs(placed[-1], own, far, bias)
    for k in range(shared, 0, -1):
        for other in arrived:
            logs = join(logs, other[:, owned << (k - 1) : owned << k])
        arrived.append(flip(logs, masks[k - 1]))
        logs = next_logs(sources.shape[0], placed[k - 1], lhs)
    for other in arrived:
        logs = join(logs, other[:, :owned])
    wide = sources.astype(jnp.float32)
    return 0.5 * jnp.sum(wide * wide, axis=0) - (1.0 / RATE) * logs[0]


def solution(mesh):
    in_specs = (P(None, ("src", "tgt")), P("src", "tgt"), P("tgt"), P("tgt"))
    out_specs = P(("src", "tgt"))
    return jax.shard_map(
        on_device, mesh=mesh, in_specs=in_specs, out_specs=out_specs, check_vma=False
    )
```

```python
import functools
import math

import jax
import jax.numpy as jnp
from jax import lax
from jax.experimental import pallas as pl
from jax.experimental.pallas import tpu as pltpu
from jax.sharding import PartitionSpec as P

EPSILON = 0.05
RATE = 1.0 / (EPSILON * math.log(2.0))
AXES = ("src", "tgt")
LANES = 128
CHUNK = 128
WIDE = 512
VMEM = pl.BlockSpec(memory_space=pltpu.VMEM)
ANY = pl.BlockSpec(memory_space=pl.ANY)


def flip(value, mask):
    n = lax.axis_size("src") * lax.axis_size("tgt")
    return lax.ppermute(value, AXES, [(i, i ^ mask) for i in range(n)])


def split3(value):
    first = value.astype(jnp.bfloat16).astype(jnp.float32)
    rest = value - first
    second = rest.astype(jnp.bfloat16).astype(jnp.float32)
    third = (rest - second).astype(jnp.bfloat16).astype(jnp.float32)
    return first, second, third


def load_kernel(sources, targets, potentials, log_mass, sources_here, targets_here, bias, scratch, sems):
    copies = [
        pltpu.make_async_copy(potentials, scratch.at[0], sems.at[0]),
        pltpu.make_async_copy(log_mass, scratch.at[1], sems.at[1]),
        pltpu.make_async_copy(sources, sources_here, sems.at[2]),
        pltpu.make_async_copy(targets, targets_here, sems.at[3]),
    ]
    for copy in copies:
        copy.start()
    copies[0].wait()
    copies[1].wait()
    bias[...] = scratch[0] + EPSILON * scratch[1]
    copies[2].wait()
    copies[3].wait()


def load(sources, targets, potentials, log_mass):
    rows = potentials.shape[0] // LANES
    return pl.pallas_call(
        load_kernel,
        out_shape=(
            pltpu.VMEM(sources.shape, sources.dtype),
            pltpu.VMEM(targets.shape, targets.dtype),
            pltpu.VMEM((rows, LANES), jnp.float32),
        ),
        in_specs=[ANY] * 4,
        out_specs=(VMEM,) * 3,
        scratch_shapes=[pltpu.VMEM((2, rows, LANES), jnp.float32), pltpu.SemaphoreType.DMA((4,))],
    )(sources, targets, potentials.reshape(rows, LANES), log_mass.reshape(rows, LANES))


def place_targets(turn, tgt_own, tgt_far, bias_ref, lhs):
    count = tgt_own.shape[1]
    width = tgt_own.shape[0] + tgt_far.shape[0]
    step = min(1024, count)
    for start in range(0, count, step):
        cols = slice(start, start + step)
        halves = [tgt_own[:, cols], tgt_far[:, cols]]
        points = jnp.concatenate(halves if start < turn else halves[::-1], axis=0)
        wide = points.astype(jnp.float32)
        half = 0.5 * jnp.sum(wide * wide, axis=0, keepdims=True)
        first, second, third = split3(bias_ref[:, cols] - half)
        place = lax.broadcasted_iota(jnp.int32, (LANES - width, step), 0)
        extra = jnp.where(place < 6, 1.0, 0.0)
        for k, part in enumerate((first, second, third)):
            extra = jnp.where(place == k, part, extra)
        lhs[cols, :] = jnp.concatenate([points, extra.astype(jnp.bfloat16)], axis=0).T


def place_sources(order, src_ref, rhs):
    width, rows = src_ref.shape
    points = src_ref[...].astype(jnp.float32)
    me = lax.axis_index("src")
    n_src = len(order)
    part = width // n_src
    blocks = [points[k * part : (k + 1) * part] for k in range(n_src)]
    for bit in range(n_src.bit_length() - 1):
        turned = ((me >> bit) & 1) == 1
        blocks = [jnp.where(turned, blocks[k ^ (1 << bit)], blocks[k]) for k in range(n_src)]
    points = jnp.concatenate([blocks[k] for k in order], axis=0)
    rhs[:width, :] = points.astype(jnp.bfloat16)
    place = lax.broadcasted_iota(jnp.int32, (LANES - width, rows), 0)
    rhs[width:, :] = jnp.where(place < 3, 1.0, 0.0).astype(jnp.bfloat16)


def sources_kernel(order, *refs):
    count = len(refs) // 2
    for src_ref, rhs in zip(refs[:count], refs[count:], strict=True):
        place_sources(order, src_ref, rhs)


def placed_sources(order, held):
    return pl.pallas_call(
        functools.partial(sources_kernel, order),
        out_shape=tuple(pltpu.VMEM((LANES, piece.shape[1]), jnp.bfloat16) for piece in held),
        in_specs=[VMEM] * len(held),
        out_specs=(VMEM,) * len(held),
        cost_estimate=pl.CostEstimate(flops=4 << 30, bytes_accessed=0, transcendentals=0),
        compiler_params=pltpu.CompilerParams(vmem_limit_bytes=8 << 20),
    )(*held)


def log_sums(width, lhs, rhs, out_ref):
    count, rows = lhs.shape[0], rhs.shape[1]

    def product(j, block):
        chunk = pl.ds(pl.multiple_of(j * CHUNK, CHUNK), CHUNK)
        found = jnp.dot(lhs[chunk, :], block, preferred_element_type=jnp.float32)
        return found.reshape(CHUNK // 8, 8, found.shape[1])

    place = lax.broadcasted_iota(jnp.int32, (LANES - width, WIDE), 0)
    for start in range(0, rows, WIDE):
        cols = slice(start, start + WIDE)
        high = jnp.max(jnp.max(product(0, rhs[:, cols]), axis=0), axis=0, keepdims=True)
        extra = jnp.where(place < 3, 1.0, 0.0)
        for k, part in enumerate(split3(-high)):
            extra = jnp.where(place == 3 + k, part, extra)
        rhs[width:, cols] = extra.astype(jnp.bfloat16)
        out_ref[:, cols] = high * RATE
    worst = jnp.zeros((1, WIDE), jnp.float32)
    for start in range(0, rows, WIDE):
        cols = slice(start, start + WIDE)
        block = rhs[:, cols]
        total = jnp.zeros((8, WIDE), jnp.float32)
        for j in range(count // CHUNK):
            total = total + jnp.sum(jnp.exp2(product(j, block) * RATE), axis=0)
        row_sum = jnp.sum(total, axis=0, keepdims=True)
        out_ref[:, cols] += jnp.log2(row_sum)
        worst = jnp.maximum(worst, row_sum)

    @pl.when(jnp.logical_not(jnp.max(worst) < jnp.inf))
    def _():
        for start in range(0, rows, WIDE):
            cols = slice(start, start + WIDE)
            extra = jnp.where(place < 3, 1.0, 0.0)
            rhs[width:, cols] = extra.astype(jnp.bfloat16)
            block = rhs[:, cols]

            def step(j, carry):
                top, total = carry
                scores = product(j, block) * RATE
                higher = jnp.maximum(top, jnp.max(scores, axis=0))
                total = total * jnp.exp2(top - higher) + jnp.sum(jnp.exp2(scores - higher[None]), axis=0)
                return higher, total

            first = jnp.max(product(0, block) * RATE, axis=0)
            top, total = lax.fori_loop(0, count // CHUNK, step, (first, jnp.zeros_like(first)))
            row_top = jnp.max(top, axis=0, keepdims=True)
            row_sum = jnp.sum(total * jnp.exp2(top - row_top), axis=0, keepdims=True)
            out_ref[:, cols] = row_top + jnp.log2(row_sum)


def first_kernel(turn, placed, tgt_own, tgt_far, bias_ref, out_ref, lhs, rhs):
    place_targets(turn, tgt_own, tgt_far, bias_ref, lhs)
    rhs[...] = placed[...]
    log_sums(tgt_own.shape[0] + tgt_far.shape[0], lhs, rhs, out_ref)


def next_kernel(width, placed, lhs, out_ref, rhs):
    rhs[...] = placed[...]
    log_sums(width, lhs, rhs, out_ref)


def estimate(rows, count):
    return pl.CostEstimate(flops=2 * rows * count * LANES, bytes_accessed=2 * count * LANES, transcendentals=rows * count)


def first_logs(turn, placed, tgt_own, tgt_far, bias):
    count, rows = tgt_own.shape[1], placed.shape[1]
    return pl.pallas_call(
        functools.partial(first_kernel, turn),
        out_shape=(pltpu.VMEM((1, rows), jnp.float32), pltpu.VMEM((count, LANES), jnp.bfloat16)),
        in_specs=[VMEM] * 4,
        out_specs=(VMEM, VMEM),
        scratch_shapes=[pltpu.VMEM((LANES, rows), jnp.bfloat16)],
        cost_estimate=estimate(rows, count),
        compiler_params=pltpu.CompilerParams(vmem_limit_bytes=48 << 20),
    )(placed, tgt_own, tgt_far, bias)


def next_logs(width, placed, lhs):
    count, rows = lhs.shape[0], placed.shape[1]
    return pl.pallas_call(
        functools.partial(next_kernel, width),
        out_shape=pltpu.VMEM((1, rows), jnp.float32),
        in_specs=[VMEM] * 2,
        out_specs=VMEM,
        scratch_shapes=[pltpu.VMEM((LANES, rows), jnp.bfloat16)],
        cost_estimate=estimate(rows, count),
        compiler_params=pltpu.CompilerParams(vmem_limit_bytes=48 << 20),
    )(placed, lhs)


def join(left, right):
    top = jnp.maximum(left, right)
    return top + jnp.log2(1.0 + jnp.exp2(-jnp.abs(left - right)))


def gather(value, masks, axis):
    for mask in masks:
        value = jnp.concatenate([value, flip(value, mask)], axis=axis)
    return value


def on_device(sources, targets, potentials, log_mass):
    n_src, n_tgt = lax.axis_size("src"), lax.axis_size("tgt")
    src_bits, tgt_bits = n_src.bit_length() - 1, n_tgt.bit_length() - 1
    shared = min(2, tgt_bits)
    masks = [(1 << bit) | n_tgt for bit in range(shared - 1, -1, -1)]
    col_masks = [1 << bit for bit in range(tgt_bits - 1, shared - 1, -1)]
    row_masks = [n_tgt << bit for bit in range(1, src_bits)]

    sources_here, targets_here, bias = load(sources, targets, potentials, log_mass)
    held = [sources]
    for mask in masks:
        whole = sources if len(held) == 1 else jnp.concatenate([sources_here, *held[1:]], axis=1)
        held.append(flip(whole, mask))
    held[0] = sources_here
    if len(col_masks) == 1 and len(row_masks) == 1:
        col_mask, row_mask = col_masks[0] | n_tgt, row_masks[0] | n_tgt
        beside = flip(targets, col_mask)
        below = flip(targets, row_mask)
        corner = flip(beside, row_mask)
        bias, _ = lax.optimization_barrier((bias, whole))
        there = flip(bias, col_mask)
        there, held[-1] = lax.optimization_barrier((there, held[-1]))
        bias = jnp.concatenate([bias, there], axis=0)
        upper = jnp.concatenate([targets_here, beside], axis=1)
        lower = jnp.concatenate([below, corner], axis=1)
        own = jnp.concatenate([upper, lower], axis=0)
        order, turn = (0, 3, 1, 2), targets.shape[1]
    else:
        own = gather(gather(targets_here, col_masks, 1), row_masks, 0)
        bias = gather(bias, col_masks, 0)
        order, turn = (*range(0, n_src, 2), *range(1, n_src, 2)), own.shape[1]
    bias = bias.reshape(1, -1)
    far = flip(own, n_tgt)
    placed = placed_sources(order, held)

    owned = sources.shape[1]
    arrived = []
    logs, lhs = first_logs(turn, placed[-1], own, far, bias)
    for k in range(shared, 0, -1):
        for other in arrived:
            logs = join(logs, other[:, owned << (k - 1) : owned << k])
        arrived.append(flip(logs, masks[k - 1]))
        logs = next_logs(sources.shape[0], placed[k - 1], lhs)
    for other in arrived:
        logs = join(logs, other[:, :owned])
    wide = sources.astype(jnp.float32)
    return 0.5 * jnp.sum(wide * wide, axis=0) - (1.0 / RATE) * logs[0]


def solution(mesh):
    in_specs = (P(None, ("src", "tgt")), P("src", "tgt"), P("tgt"), P("tgt"))
    out_specs = P(("src", "tgt"))
    return jax.shard_map(
        on_device, mesh=mesh, in_specs=in_specs, out_specs=out_specs, check_vma=False
    )
```

```python
import functools
import math

import jax
import jax.numpy as jnp
from jax import lax
from jax.experimental import pallas as pl
from jax.experimental.pallas import tpu as pltpu
from jax.sharding import PartitionSpec as P

EPSILON = 0.05
RATE = 1.0 / (EPSILON * math.log(2.0))
AXES = ("src", "tgt")
LANES = 128
CHUNK = 128
WIDE = 512
VMEM = pl.BlockSpec(memory_space=pltpu.VMEM)
ANY = pl.BlockSpec(memory_space=pl.ANY)


def flip(value, mask):
    n = lax.axis_size("src") * lax.axis_size("tgt")
    return lax.ppermute(value, AXES, [(i, i ^ mask) for i in range(n)])


def split3(value):
    first = value.astype(jnp.bfloat16).astype(jnp.float32)
    rest = value - first
    second = rest.astype(jnp.bfloat16).astype(jnp.float32)
    third = (rest - second).astype(jnp.bfloat16).astype(jnp.float32)
    return first, second, third


def load_kernel(sources, targets, potentials, log_mass, sources_here, targets_here, bias, scratch, sems):
    copies = [
        pltpu.make_async_copy(potentials, scratch.at[0], sems.at[0]),
        pltpu.make_async_copy(log_mass, scratch.at[1], sems.at[1]),
        pltpu.make_async_copy(sources, sources_here, sems.at[2]),
        pltpu.make_async_copy(targets, targets_here, sems.at[3]),
    ]
    for copy in copies:
        copy.start()
    copies[0].wait()
    copies[1].wait()
    bias[...] = scratch[0] + EPSILON * scratch[1]
    copies[2].wait()
    copies[3].wait()


def load(sources, targets, potentials, log_mass):
    rows = potentials.shape[0] // LANES
    return pl.pallas_call(
        load_kernel,
        out_shape=(
            pltpu.VMEM(sources.shape, sources.dtype),
            pltpu.VMEM(targets.shape, targets.dtype),
            pltpu.VMEM((rows, LANES), jnp.float32),
        ),
        in_specs=[ANY] * 4,
        out_specs=(VMEM,) * 3,
        scratch_shapes=[pltpu.VMEM((2, rows, LANES), jnp.float32), pltpu.SemaphoreType.DMA((4,))],
    )(sources, targets, potentials.reshape(rows, LANES), log_mass.reshape(rows, LANES))


def place_targets(turn, tgt_own, tgt_far, bias_ref, lhs):
    count = tgt_own.shape[1]
    width = tgt_own.shape[0] + tgt_far.shape[0]
    step = min(1024, count)
    for start in range(0, count, step):
        cols = slice(start, start + step)
        halves = [tgt_own[:, cols], tgt_far[:, cols]]
        points = jnp.concatenate(halves if start < turn else halves[::-1], axis=0)
        wide = points.astype(jnp.float32)
        half = 0.5 * jnp.sum(wide * wide, axis=0, keepdims=True)
        first, second, third = split3(bias_ref[:, cols] - half)
        place = lax.broadcasted_iota(jnp.int32, (LANES - width, step), 0)
        extra = jnp.where(place < 6, 1.0, 0.0)
        for k, part in enumerate((first, second, third)):
            extra = jnp.where(place == k, part, extra)
        lhs[cols, :] = jnp.concatenate([points, extra.astype(jnp.bfloat16)], axis=0).T


def place_sources(order, src_ref, rhs):
    width, rows = src_ref.shape
    points = src_ref[...].astype(jnp.float32)
    me = lax.axis_index("src")
    n_src = len(order)
    part = width // n_src
    blocks = [points[k * part : (k + 1) * part] for k in range(n_src)]
    for bit in range(n_src.bit_length() - 1):
        turned = ((me >> bit) & 1) == 1
        blocks = [jnp.where(turned, blocks[k ^ (1 << bit)], blocks[k]) for k in range(n_src)]
    points = jnp.concatenate([blocks[k] for k in order], axis=0)
    rhs[:width, :] = points.astype(jnp.bfloat16)
    place = lax.broadcasted_iota(jnp.int32, (LANES - width, rows), 0)
    rhs[width:, :] = jnp.where(place < 3, 1.0, 0.0).astype(jnp.bfloat16)


def sources_kernel(order, *refs):
    count = len(refs) // 2
    for src_ref, rhs in zip(refs[:count], refs[count:], strict=True):
        place_sources(order, src_ref, rhs)


def placed_sources(order, held):
    return pl.pallas_call(
        functools.partial(sources_kernel, order),
        out_shape=tuple(pltpu.VMEM((LANES, piece.shape[1]), jnp.bfloat16) for piece in held),
        in_specs=[VMEM] * len(held),
        out_specs=(VMEM,) * len(held),
        cost_estimate=pl.CostEstimate(flops=1 << 30, bytes_accessed=0, transcendentals=0),
        compiler_params=pltpu.CompilerParams(vmem_limit_bytes=8 << 20),
    )(*held)


def log_sums(width, lhs, rhs, out_ref):
    count, rows = lhs.shape[0], rhs.shape[1]

    def product(j, block):
        chunk = pl.ds(pl.multiple_of(j * CHUNK, CHUNK), CHUNK)
        found = jnp.dot(lhs[chunk, :], block, preferred_element_type=jnp.float32)
        return found.reshape(CHUNK // 8, 8, found.shape[1])

    place = lax.broadcasted_iota(jnp.int32, (LANES - width, WIDE), 0)
    for start in range(0, rows, WIDE):
        cols = slice(start, start + WIDE)
        high = jnp.max(jnp.max(product(0, rhs[:, cols]), axis=0), axis=0, keepdims=True)
        extra = jnp.where(place < 3, 1.0, 0.0)
        for k, part in enumerate(split3(-high)):
            extra = jnp.where(place == 3 + k, part, extra)
        rhs[width:, cols] = extra.astype(jnp.bfloat16)
        out_ref[:, cols] = high * RATE
    worst = jnp.zeros((1, WIDE), jnp.float32)
    for start in range(0, rows, WIDE):
        cols = slice(start, start + WIDE)
        block = rhs[:, cols]
        total = jnp.zeros((8, WIDE), jnp.float32)
        for j in range(count // CHUNK):
            total = total + jnp.sum(jnp.exp2(product(j, block) * RATE), axis=0)
        row_sum = jnp.sum(total, axis=0, keepdims=True)
        out_ref[:, cols] += jnp.log2(row_sum)
        worst = jnp.maximum(worst, row_sum)

    @pl.when(jnp.logical_not(jnp.max(worst) < jnp.inf))
    def _():
        for start in range(0, rows, WIDE):
            cols = slice(start, start + WIDE)
            extra = jnp.where(place < 3, 1.0, 0.0)
            rhs[width:, cols] = extra.astype(jnp.bfloat16)
            block = rhs[:, cols]

            def step(j, carry):
                top, total = carry
                scores = product(j, block) * RATE
                higher = jnp.maximum(top, jnp.max(scores, axis=0))
                total = total * jnp.exp2(top - higher) + jnp.sum(jnp.exp2(scores - higher[None]), axis=0)
                return higher, total

            first = jnp.max(product(0, block) * RATE, axis=0)
            top, total = lax.fori_loop(0, count // CHUNK, step, (first, jnp.zeros_like(first)))
            row_top = jnp.max(top, axis=0, keepdims=True)
            row_sum = jnp.sum(total * jnp.exp2(top - row_top), axis=0, keepdims=True)
            out_ref[:, cols] = row_top + jnp.log2(row_sum)


def first_kernel(turn, placed, tgt_own, tgt_far, bias_ref, out_ref, lhs, rhs):
    place_targets(turn, tgt_own, tgt_far, bias_ref, lhs)
    rhs[...] = placed[...]
    log_sums(tgt_own.shape[0] + tgt_far.shape[0], lhs, rhs, out_ref)


def next_kernel(width, placed, lhs, out_ref, rhs):
    rhs[...] = placed[...]
    log_sums(width, lhs, rhs, out_ref)


def estimate(rows, count):
    return pl.CostEstimate(flops=2 * rows * count * LANES, bytes_accessed=2 * count * LANES, transcendentals=rows * count)


def first_logs(turn, placed, tgt_own, tgt_far, bias):
    count, rows = tgt_own.shape[1], placed.shape[1]
    return pl.pallas_call(
        functools.partial(first_kernel, turn),
        out_shape=(pltpu.VMEM((1, rows), jnp.float32), pltpu.VMEM((count, LANES), jnp.bfloat16)),
        in_specs=[VMEM] * 4,
        out_specs=(VMEM, VMEM),
        scratch_shapes=[pltpu.VMEM((LANES, rows), jnp.bfloat16)],
        cost_estimate=estimate(rows, count),
        compiler_params=pltpu.CompilerParams(vmem_limit_bytes=48 << 20),
    )(placed, tgt_own, tgt_far, bias)


def next_logs(width, placed, lhs):
    count, rows = lhs.shape[0], placed.shape[1]
    return pl.pallas_call(
        functools.partial(next_kernel, width),
        out_shape=pltpu.VMEM((1, rows), jnp.float32),
        in_specs=[VMEM] * 2,
        out_specs=VMEM,
        scratch_shapes=[pltpu.VMEM((LANES, rows), jnp.bfloat16)],
        cost_estimate=estimate(rows, count),
        compiler_params=pltpu.CompilerParams(vmem_limit_bytes=48 << 20),
    )(placed, lhs)


def join(left, right):
    top = jnp.maximum(left, right)
    return top + jnp.log2(1.0 + jnp.exp2(-jnp.abs(left - right)))


def gather(value, masks, axis):
    for mask in masks:
        value = jnp.concatenate([value, flip(value, mask)], axis=axis)
    return value


def on_device(sources, targets, potentials, log_mass):
    n_src, n_tgt = lax.axis_size("src"), lax.axis_size("tgt")
    src_bits, tgt_bits = n_src.bit_length() - 1, n_tgt.bit_length() - 1
    shared = min(2, tgt_bits)
    masks = [(1 << bit) | n_tgt for bit in range(shared - 1, -1, -1)]
    col_masks = [1 << bit for bit in range(tgt_bits - 1, shared - 1, -1)]
    row_masks = [n_tgt << bit for bit in range(1, src_bits)]

    sources_here, targets_here, bias = load(sources, targets, potentials, log_mass)
    held = [sources]
    for mask in masks:
        whole = sources if len(held) == 1 else jnp.concatenate([sources_here, *held[1:]], axis=1)
        held.append(flip(whole, mask))
    held[0] = sources_here
    if len(col_masks) == 1 and len(row_masks) == 1:
        col_mask, row_mask = col_masks[0] | n_tgt, row_masks[0] | n_tgt
        beside = flip(targets, col_mask)
        below = flip(targets, row_mask)
        corner = flip(beside, row_mask)
        bias, _ = lax.optimization_barrier((bias, held[1]))
        there = flip(bias, col_mask)
        there, held[-1] = lax.optimization_barrier((there, held[-1]))
        bias = jnp.concatenate([bias, there], axis=0)
        upper = jnp.concatenate([targets_here, beside], axis=1)
        lower = jnp.concatenate([below, corner], axis=1)
        own = jnp.concatenate([upper, lower], axis=0)
        order, turn = (0, 3, 1, 2), targets.shape[1]
    else:
        own = gather(gather(targets_here, col_masks, 1), row_masks, 0)
        bias = gather(bias, col_masks, 0)
        order, turn = (*range(0, n_src, 2), *range(1, n_src, 2)), own.shape[1]
    bias = bias.reshape(1, -1)
    far = flip(own, n_tgt)
    placed = placed_sources(order, held)

    owned = sources.shape[1]
    arrived = []
    logs, lhs = first_logs(turn, placed[-1], own, far, bias)
    for k in range(shared, 0, -1):
        for other in arrived:
            logs = join(logs, other[:, owned << (k - 1) : owned << k])
        arrived.append(flip(logs, masks[k - 1]))
        logs = next_logs(sources.shape[0], placed[k - 1], lhs)
    for other in arrived:
        logs = join(logs, other[:, :owned])
    wide = sources.astype(jnp.float32)
    return 0.5 * jnp.sum(wide * wide, axis=0) - (1.0 / RATE) * logs[0]


def solution(mesh):
    in_specs = (P(None, ("src", "tgt")), P("src", "tgt"), P("tgt"), P("tgt"))
    out_specs = P(("src", "tgt"))
    return jax.shard_map(
        on_device, mesh=mesh, in_specs=in_specs, out_specs=out_specs, check_vma=False
    )
```

```python
import functools
import math

import jax
import jax.numpy as jnp
from jax import lax
from jax.experimental import pallas as pl
from jax.experimental.pallas import tpu as pltpu
from jax.sharding import PartitionSpec as P

EPSILON = 0.05
RATE = 1.0 / (EPSILON * math.log(2.0))
AXES = ("src", "tgt")
LANES = 128
CHUNK = 128
WIDE = 512
VMEM = pl.BlockSpec(memory_space=pltpu.VMEM)
ANY = pl.BlockSpec(memory_space=pl.ANY)


def flip(value, mask):
    n = lax.axis_size("src") * lax.axis_size("tgt")
    return lax.ppermute(value, AXES, [(i, i ^ mask) for i in range(n)])


def split3(value):
    first = value.astype(jnp.bfloat16).astype(jnp.float32)
    rest = value - first
    second = rest.astype(jnp.bfloat16).astype(jnp.float32)
    third = (rest - second).astype(jnp.bfloat16).astype(jnp.float32)
    return first, second, third


def load_kernel(sources, targets, potentials, log_mass, sources_here, targets_here, bias, scratch, sems):
    copies = [
        pltpu.make_async_copy(potentials, scratch.at[0], sems.at[0]),
        pltpu.make_async_copy(log_mass, scratch.at[1], sems.at[1]),
        pltpu.make_async_copy(sources, sources_here, sems.at[2]),
        pltpu.make_async_copy(targets, targets_here, sems.at[3]),
    ]
    for copy in copies:
        copy.start()
    copies[0].wait()
    copies[1].wait()
    bias[...] = scratch[0] + EPSILON * scratch[1]
    copies[2].wait()
    copies[3].wait()


def load(sources, targets, potentials, log_mass):
    rows = potentials.shape[0] // LANES
    return pl.pallas_call(
        load_kernel,
        out_shape=(
            pltpu.VMEM(sources.shape, sources.dtype),
            pltpu.VMEM(targets.shape, targets.dtype),
            pltpu.VMEM((rows, LANES), jnp.float32),
        ),
        in_specs=[ANY] * 4,
        out_specs=(VMEM,) * 3,
        scratch_shapes=[pltpu.VMEM((2, rows, LANES), jnp.float32), pltpu.SemaphoreType.DMA((4,))],
    )(sources, targets, potentials.reshape(rows, LANES), log_mass.reshape(rows, LANES))


def place_targets(tgt_own, tgt_far, bias_ref, lhs):
    count = tgt_own.shape[1]
    width = tgt_own.shape[0] + tgt_far.shape[0]
    step = min(1024, count)
    for start in range(0, count, step):
        cols = slice(start, start + step)
        points = jnp.concatenate([tgt_own[:, cols], tgt_far[:, cols]], axis=0)
        wide = points.astype(jnp.float32)
        half = 0.5 * jnp.sum(wide * wide, axis=0, keepdims=True)
        first, second, third = split3(bias_ref[:, cols] - half)
        place = lax.broadcasted_iota(jnp.int32, (LANES - width, step), 0)
        extra = jnp.where(place < 6, 1.0, 0.0)
        for k, part in enumerate((first, second, third)):
            extra = jnp.where(place == k, part, extra)
        lhs[cols, :] = jnp.concatenate([points, extra.astype(jnp.bfloat16)], axis=0).T


def place_sources(order, src_ref, rhs):
    width, rows = src_ref.shape
    points = src_ref[...].astype(jnp.float32)
    me = lax.axis_index("src")
    n_src = len(order)
    part = width // n_src
    blocks = [points[k * part : (k + 1) * part] for k in range(n_src)]
    for bit in range(n_src.bit_length() - 1):
        turned = ((me >> bit) & 1) == 1
        blocks = [jnp.where(turned, blocks[k ^ (1 << bit)], blocks[k]) for k in range(n_src)]
    points = jnp.concatenate([blocks[k] for k in order], axis=0)
    rhs[:width, :] = points.astype(jnp.bfloat16)
    place = lax.broadcasted_iota(jnp.int32, (LANES - width, rows), 0)
    rhs[width:, :] = jnp.where(place < 3, 1.0, 0.0).astype(jnp.bfloat16)


def sources_kernel(order, *refs):
    count = len(refs) // 2
    for src_ref, rhs in zip(refs[:count], refs[count:], strict=True):
        place_sources(order, src_ref, rhs)


def placed_sources(order, held):
    return pl.pallas_call(
        functools.partial(sources_kernel, order),
        out_shape=tuple(pltpu.VMEM((LANES, piece.shape[1]), jnp.bfloat16) for piece in held),
        in_specs=[VMEM] * len(held),
        out_specs=(VMEM,) * len(held),
        cost_estimate=pl.CostEstimate(flops=1 << 30, bytes_accessed=0, transcendentals=0),
        compiler_params=pltpu.CompilerParams(vmem_limit_bytes=8 << 20),
    )(*held)


def log_sums(width, lhs, rhs, out_ref):
    count, rows = lhs.shape[0], rhs.shape[1]

    def product(j, block):
        chunk = pl.ds(pl.multiple_of(j * CHUNK, CHUNK), CHUNK)
        found = jnp.dot(lhs[chunk, :], block, preferred_element_type=jnp.float32)
        return found.reshape(CHUNK // 8, 8, found.shape[1])

    place = lax.broadcasted_iota(jnp.int32, (LANES - width, WIDE), 0)
    for start in range(0, rows, WIDE):
        cols = slice(start, start + WIDE)
        high = jnp.max(jnp.max(product(0, rhs[:, cols]), axis=0), axis=0, keepdims=True)
        extra = jnp.where(place < 3, 1.0, 0.0)
        for k, part in enumerate(split3(-high)):
            extra = jnp.where(place == 3 + k, part, extra)
        rhs[width:, cols] = extra.astype(jnp.bfloat16)
        out_ref[:, cols] = high * RATE
    worst = jnp.zeros((1, WIDE), jnp.float32)
    for start in range(0, rows, WIDE):
        cols = slice(start, start + WIDE)
        block = rhs[:, cols]
        total = jnp.zeros((8, WIDE), jnp.float32)
        for j in range(count // CHUNK):
            total = total + jnp.sum(jnp.exp2(product(j, block) * RATE), axis=0)
        row_sum = jnp.sum(total, axis=0, keepdims=True)
        out_ref[:, cols] += jnp.log2(row_sum)
        worst = jnp.maximum(worst, row_sum)

    @pl.when(jnp.logical_not(jnp.max(worst) < jnp.inf))
    def _():
        for start in range(0, rows, WIDE):
            cols = slice(start, start + WIDE)
            extra = jnp.where(place < 3, 1.0, 0.0)
            rhs[width:, cols] = extra.astype(jnp.bfloat16)
            block = rhs[:, cols]

            def step(j, carry):
                top, total = carry
                scores = product(j, block) * RATE
                higher = jnp.maximum(top, jnp.max(scores, axis=0))
                total = total * jnp.exp2(top - higher) + jnp.sum(jnp.exp2(scores - higher[None]), axis=0)
                return higher, total

            first = jnp.max(product(0, block) * RATE, axis=0)
            top, total = lax.fori_loop(0, count // CHUNK, step, (first, jnp.zeros_like(first)))
            row_top = jnp.max(top, axis=0, keepdims=True)
            row_sum = jnp.sum(total * jnp.exp2(top - row_top), axis=0, keepdims=True)
            out_ref[:, cols] = row_top + jnp.log2(row_sum)


def first_kernel(placed, tgt_own, tgt_far, bias_ref, out_ref, lhs, rhs):
    place_targets(tgt_own, tgt_far, bias_ref, lhs)
    rhs[...] = placed[...]
    log_sums(tgt_own.shape[0] + tgt_far.shape[0], lhs, rhs, out_ref)


def next_kernel(width, placed, lhs, out_ref, rhs):
    rhs[...] = placed[...]
    log_sums(width, lhs, rhs, out_ref)


def estimate(rows, count):
    return pl.CostEstimate(flops=2 * rows * count * LANES, bytes_accessed=2 * count * LANES, transcendentals=rows * count)


def first_logs(placed, tgt_own, tgt_far, bias):
    count, rows = tgt_own.shape[1], placed.shape[1]
    return pl.pallas_call(
        first_kernel,
        out_shape=(pltpu.VMEM((1, rows), jnp.float32), pltpu.VMEM((count, LANES), jnp.bfloat16)),
        in_specs=[VMEM] * 4,
        out_specs=(VMEM, VMEM),
        scratch_shapes=[pltpu.VMEM((LANES, rows), jnp.bfloat16)],
        cost_estimate=estimate(rows, count),
        compiler_params=pltpu.CompilerParams(vmem_limit_bytes=48 << 20),
    )(placed, tgt_own, tgt_far, bias)


def next_logs(width, placed, lhs):
    count, rows = lhs.shape[0], placed.shape[1]
    return pl.pallas_call(
        functools.partial(next_kernel, width),
        out_shape=pltpu.VMEM((1, rows), jnp.float32),
        in_specs=[VMEM] * 2,
        out_specs=VMEM,
        scratch_shapes=[pltpu.VMEM((LANES, rows), jnp.bfloat16)],
        cost_estimate=estimate(rows, count),
        compiler_params=pltpu.CompilerParams(vmem_limit_bytes=48 << 20),
    )(placed, lhs)


def join(left, right):
    top = jnp.maximum(left, right)
    return top + jnp.log2(1.0 + jnp.exp2(-jnp.abs(left - right)))


def gather(value, masks, axis):
    for mask in masks:
        value = jnp.concatenate([value, flip(value, mask)], axis=axis)
    return value


def on_device(sources, targets, potentials, log_mass):
    n_src, n_tgt = lax.axis_size("src"), lax.axis_size("tgt")
    src_bits, tgt_bits = n_src.bit_length() - 1, n_tgt.bit_length() - 1
    shared = min(2, tgt_bits)
    masks = [(1 << bit) | n_tgt for bit in range(shared - 1, -1, -1)]
    col_masks = [1 << bit for bit in range(tgt_bits - 1, shared - 1, -1)]
    row_masks = [n_tgt << bit for bit in range(1, src_bits)]

    sources_here, targets_here, bias = load(sources, targets, potentials, log_mass)
    held = [sources]
    for mask in masks:
        whole = sources if len(held) == 1 else jnp.concatenate([sources_here, *held[1:]], axis=1)
        held.append(flip(whole, mask))
    held[0] = sources_here
    if len(col_masks) == 1 and len(row_masks) == 1:
        beside = flip(targets, col_masks[0])
        below = flip(targets, row_masks[0])
        corner = flip(beside, row_masks[0])
        bias, _ = lax.optimization_barrier((bias, held[1]))
        there = flip(bias, col_masks[0])
        there, held[-1] = lax.optimization_barrier((there, held[-1]))
        bias = jnp.concatenate([bias, there], axis=0)
        upper = jnp.concatenate([targets_here, beside], axis=1)
        lower = jnp.concatenate([below, corner], axis=1)
        own = jnp.concatenate([upper, lower], axis=0)
    else:
        own = gather(gather(targets_here, col_masks, 1), row_masks, 0)
        bias = gather(bias, col_masks, 0)
    bias = bias.reshape(1, -1)
    far = flip(own, n_tgt)
    order = (*range(0, n_src, 2), *range(1, n_src, 2))
    placed = placed_sources(order, held)

    owned = sources.shape[1]
    arrived = []
    logs, lhs = first_logs(placed[-1], own, far, bias)
    for k in range(shared, 0, -1):
        for other in arrived:
            logs = join(logs, other[:, owned << (k - 1) : owned << k])
        arrived.append(flip(logs, masks[k - 1]))
        logs = next_logs(sources.shape[0], placed[k - 1], lhs)
    for other in arrived:
        logs = join(logs, other[:, :owned])
    wide = sources.astype(jnp.float32)
    return 0.5 * jnp.sum(wide * wide, axis=0) - (1.0 / RATE) * logs[0]


def solution(mesh):
    in_specs = (P(None, ("src", "tgt")), P("src", "tgt"), P("tgt"), P("tgt"))
    out_specs = P(("src", "tgt"))
    return jax.shard_map(
        on_device, mesh=mesh, in_specs=in_specs, out_specs=out_specs, check_vma=False
    )
```

```python
import functools
import math

import jax
import jax.numpy as jnp
from jax import lax
from jax.experimental import pallas as pl
from jax.experimental.pallas import tpu as pltpu
from jax.sharding import PartitionSpec as P

EPSILON = 0.05
RATE = 1.0 / (EPSILON * math.log(2.0))
AXES = ("src", "tgt")
LANES = 128
CHUNK = 128
WIDE = 512
VMEM = pl.BlockSpec(memory_space=pltpu.VMEM)
ANY = pl.BlockSpec(memory_space=pl.ANY)


def flip(value, mask):
    n = lax.axis_size("src") * lax.axis_size("tgt")
    return lax.ppermute(value, AXES, [(i, i ^ mask) for i in range(n)])


def split3(value):
    first = value.astype(jnp.bfloat16).astype(jnp.float32)
    rest = value - first
    second = rest.astype(jnp.bfloat16).astype(jnp.float32)
    third = (rest - second).astype(jnp.bfloat16).astype(jnp.float32)
    return first, second, third


def load_kernel(sources, targets, potentials, log_mass, sources_here, targets_here, bias, scratch, sems):
    copies = [
        pltpu.make_async_copy(potentials, scratch.at[0], sems.at[0]),
        pltpu.make_async_copy(log_mass, scratch.at[1], sems.at[1]),
        pltpu.make_async_copy(sources, sources_here, sems.at[2]),
        pltpu.make_async_copy(targets, targets_here, sems.at[3]),
    ]
    for copy in copies:
        copy.start()
    copies[0].wait()
    copies[1].wait()
    bias[...] = scratch[0] + EPSILON * scratch[1]
    copies[2].wait()
    copies[3].wait()


def load(sources, targets, potentials, log_mass):
    rows = potentials.shape[0] // LANES
    return pl.pallas_call(
        load_kernel,
        out_shape=(
            pltpu.VMEM(sources.shape, sources.dtype),
            pltpu.VMEM(targets.shape, targets.dtype),
            pltpu.VMEM((rows, LANES), jnp.float32),
        ),
        in_specs=[ANY] * 4,
        out_specs=(VMEM,) * 3,
        scratch_shapes=[pltpu.VMEM((2, rows, LANES), jnp.float32), pltpu.SemaphoreType.DMA((4,))],
    )(sources, targets, potentials.reshape(rows, LANES), log_mass.reshape(rows, LANES))


def place_targets(tgt_own, tgt_far, bias_ref, lhs):
    count = tgt_own.shape[1]
    width = tgt_own.shape[0] + tgt_far.shape[0]
    step = min(1024, count)
    for start in range(0, count, step):
        cols = slice(start, start + step)
        points = jnp.concatenate([tgt_own[:, cols], tgt_far[:, cols]], axis=0)
        wide = points.astype(jnp.float32)
        half = 0.5 * jnp.sum(wide * wide, axis=0, keepdims=True)
        first, second, third = split3(bias_ref[:, cols] - half)
        place = lax.broadcasted_iota(jnp.int32, (LANES - width, step), 0)
        extra = jnp.where(place < 6, 1.0, 0.0)
        for k, part in enumerate((first, second, third)):
            extra = jnp.where(place == k, part, extra)
        lhs[cols, :] = jnp.concatenate([points, extra.astype(jnp.bfloat16)], axis=0).T


def place_sources(order, src_ref, rhs):
    width, rows = src_ref.shape
    points = src_ref[...].astype(jnp.float32)
    me = lax.axis_index("src")
    n_src = len(order)
    part = width // n_src
    blocks = [points[k * part : (k + 1) * part] for k in range(n_src)]
    for bit in range(n_src.bit_length() - 1):
        turned = ((me >> bit) & 1) == 1
        blocks = [jnp.where(turned, blocks[k ^ (1 << bit)], blocks[k]) for k in range(n_src)]
    points = jnp.concatenate([blocks[k] for k in order], axis=0)
    rhs[:width, :] = points.astype(jnp.bfloat16)
    place = lax.broadcasted_iota(jnp.int32, (LANES - width, rows), 0)
    rhs[width:, :] = jnp.where(place < 3, 1.0, 0.0).astype(jnp.bfloat16)


def sources_kernel(order, *refs):
    count = len(refs) // 2
    for src_ref, rhs in zip(refs[:count], refs[count:], strict=True):
        place_sources(order, src_ref, rhs)


def placed_sources(order, held):
    return pl.pallas_call(
        functools.partial(sources_kernel, order),
        out_shape=tuple(pltpu.VMEM((LANES, piece.shape[1]), jnp.bfloat16) for piece in held),
        in_specs=[VMEM] * len(held),
        out_specs=(VMEM,) * len(held),
        cost_estimate=pl.CostEstimate(flops=1 << 30, bytes_accessed=0, transcendentals=0),
        compiler_params=pltpu.CompilerParams(vmem_limit_bytes=8 << 20),
    )(*held)


def references(width, lhs, placed, out_ref):
    chunk = lhs[:CHUNK, :]
    for start in range(0, placed.shape[1], WIDE):
        cols = slice(start, start + WIDE)
        found = jnp.dot(chunk, placed[:, cols], preferred_element_type=jnp.float32)
        out_ref[:, cols] = jnp.max(jnp.max(found.reshape(CHUNK // 8, 8, WIDE), axis=0), axis=0, keepdims=True)


def log_sums(width, lhs, placed, high_ref, out_ref):
    count, rows = lhs.shape[0], placed.shape[1]
    place = lax.broadcasted_iota(jnp.int32, (LANES - width, WIDE), 0)

    def product(j, block):
        chunk = pl.ds(pl.multiple_of(j * CHUNK, CHUNK), CHUNK)
        found = jnp.dot(lhs[chunk, :], block, preferred_element_type=jnp.float32)
        return found.reshape(CHUNK // 8, 8, found.shape[1])

    worst = jnp.zeros((1, WIDE), jnp.float32)
    for start in range(0, rows, WIDE):
        cols = slice(start, start + WIDE)
        high = high_ref[:, cols]
        extra = jnp.where(place < 3, 1.0, 0.0)
        for k, part in enumerate(split3(-high)):
            extra = jnp.where(place == 3 + k, part, extra)
        block = jnp.concatenate([placed[:width, cols], extra.astype(jnp.bfloat16)], axis=0)
        total = jnp.zeros((8, WIDE), jnp.float32)
        for j in range(count // CHUNK):
            total = total + jnp.sum(jnp.exp2(product(j, block) * RATE), axis=0)
        row_sum = jnp.sum(total, axis=0, keepdims=True)
        out_ref[:, cols] = high * RATE + jnp.log2(row_sum)
        worst = jnp.maximum(worst, row_sum)

    @pl.when(jnp.logical_not(jnp.max(worst) < jnp.inf))
    def _():
        for start in range(0, rows, WIDE):
            cols = slice(start, start + WIDE)
            block = placed[:, cols]

            def step(j, carry):
                top, total = carry
                scores = product(j, block) * RATE
                higher = jnp.maximum(top, jnp.max(scores, axis=0))
                total = total * jnp.exp2(top - higher) + jnp.sum(jnp.exp2(scores - higher[None]), axis=0)
                return higher, total

            first = jnp.max(product(0, block) * RATE, axis=0)
            top, total = lax.fori_loop(0, count // CHUNK, step, (first, jnp.zeros_like(first)))
            row_top = jnp.max(top, axis=0, keepdims=True)
            row_sum = jnp.sum(total * jnp.exp2(top - row_top), axis=0, keepdims=True)
            out_ref[:, cols] = row_top + jnp.log2(row_sum)


def first_kernel(placed, tgt_own, tgt_far, bias_ref, out_ref, lhs, high):
    place_targets(tgt_own, tgt_far, bias_ref, lhs)
    width = tgt_own.shape[0] + tgt_far.shape[0]
    references(width, lhs, placed, high)
    log_sums(width, lhs, placed, high, out_ref)


def next_kernel(width, placed, lhs, out_ref, high):
    references(width, lhs, placed, high)
    log_sums(width, lhs, placed, high, out_ref)


def estimate(rows, count):
    return pl.CostEstimate(flops=2 * rows * count * LANES, bytes_accessed=2 * count * LANES, transcendentals=rows * count)


def first_logs(placed, tgt_own, tgt_far, bias):
    count, rows = tgt_own.shape[1], placed.shape[1]
    return pl.pallas_call(
        first_kernel,
        out_shape=(pltpu.VMEM((1, rows), jnp.float32), pltpu.VMEM((count, LANES), jnp.bfloat16)),
        in_specs=[VMEM] * 4,
        out_specs=(VMEM, VMEM),
        scratch_shapes=[pltpu.VMEM((1, rows), jnp.float32)],
        cost_estimate=estimate(rows, count),
        compiler_params=pltpu.CompilerParams(vmem_limit_bytes=48 << 20),
    )(placed, tgt_own, tgt_far, bias)


def next_logs(width, placed, lhs):
    count, rows = lhs.shape[0], placed.shape[1]
    return pl.pallas_call(
        functools.partial(next_kernel, width),
        out_shape=pltpu.VMEM((1, rows), jnp.float32),
        in_specs=[VMEM] * 2,
        out_specs=VMEM,
        scratch_shapes=[pltpu.VMEM((1, rows), jnp.float32)],
        cost_estimate=estimate(rows, count),
        compiler_params=pltpu.CompilerParams(vmem_limit_bytes=48 << 20),
    )(placed, lhs)


def join(left, right):
    top = jnp.maximum(left, right)
    return top + jnp.log2(1.0 + jnp.exp2(-jnp.abs(left - right)))


def gather(value, masks, axis):
    for mask in masks:
        value = jnp.concatenate([value, flip(value, mask)], axis=axis)
    return value


def on_device(sources, targets, potentials, log_mass):
    n_src, n_tgt = lax.axis_size("src"), lax.axis_size("tgt")
    src_bits, tgt_bits = n_src.bit_length() - 1, n_tgt.bit_length() - 1
    shared = min(2, tgt_bits)
    masks = [(1 << bit) | n_tgt for bit in range(shared - 1, -1, -1)]
    col_masks = [1 << bit for bit in range(tgt_bits - 1, shared - 1, -1)]
    row_masks = [n_tgt << bit for bit in range(1, src_bits)]

    sources_here, targets_here, bias = load(sources, targets, potentials, log_mass)
    held = [sources]
    for mask in masks:
        whole = sources if len(held) == 1 else jnp.concatenate([sources_here, *held[1:]], axis=1)
        held.append(flip(whole, mask))
    held[0] = sources_here
    if len(col_masks) == 1 and len(row_masks) == 1:
        beside = flip(targets, col_masks[0])
        below = flip(targets, row_masks[0])
        corner = flip(beside, row_masks[0])
        bias, _ = lax.optimization_barrier((bias, held[1]))
        there = flip(bias, col_masks[0])
        there, held[-1] = lax.optimization_barrier((there, held[-1]))
        bias = jnp.concatenate([bias, there], axis=0)
        upper = jnp.concatenate([targets_here, beside], axis=1)
        lower = jnp.concatenate([below, corner], axis=1)
        own = jnp.concatenate([upper, lower], axis=0)
    else:
        own = gather(gather(targets_here, col_masks, 1), row_masks, 0)
        bias = gather(bias, col_masks, 0)
    bias = bias.reshape(1, -1)
    far = flip(own, n_tgt)
    order = (*range(0, n_src, 2), *range(1, n_src, 2))
    placed = placed_sources(order, held)

    owned = sources.shape[1]
    arrived = []
    logs, lhs = first_logs(placed[-1], own, far, bias)
    for k in range(shared, 0, -1):
        for other in arrived:
            logs = join(logs, other[:, owned << (k - 1) : owned << k])
        arrived.append(flip(logs, masks[k - 1]))
        logs = next_logs(sources.shape[0], placed[k - 1], lhs)
    for other in arrived:
        logs = join(logs, other[:, :owned])
    wide = sources.astype(jnp.float32)
    return 0.5 * jnp.sum(wide * wide, axis=0) - (1.0 / RATE) * logs[0]


def solution(mesh):
    in_specs = (P(None, ("src", "tgt")), P("src", "tgt"), P("tgt"), P("tgt"))
    out_specs = P(("src", "tgt"))
    return jax.shard_map(
        on_device, mesh=mesh, in_specs=in_specs, out_specs=out_specs, check_vma=False
    )
```

```python
import functools
import math

import jax
import jax.numpy as jnp
from jax import lax
from jax.experimental import pallas as pl
from jax.experimental.pallas import tpu as pltpu
from jax.sharding import PartitionSpec as P

EPSILON = 0.05
RATE = 1.0 / (EPSILON * math.log(2.0))
AXES = ("src", "tgt")
LANES = 128
CHUNK = 128
WIDE = 512
VMEM = pl.BlockSpec(memory_space=pltpu.VMEM)
ANY = pl.BlockSpec(memory_space=pl.ANY)


def flip(value, mask):
    n = lax.axis_size("src") * lax.axis_size("tgt")
    return lax.ppermute(value, AXES, [(i, i ^ mask) for i in range(n)])


def split3(value):
    first = value.astype(jnp.bfloat16).astype(jnp.float32)
    rest = value - first
    second = rest.astype(jnp.bfloat16).astype(jnp.float32)
    third = (rest - second).astype(jnp.bfloat16).astype(jnp.float32)
    return first, second, third


def load_kernel(sources, targets, potentials, log_mass, sources_here, targets_here, bias, scratch, sems):
    copies = [
        pltpu.make_async_copy(potentials, scratch.at[0], sems.at[0]),
        pltpu.make_async_copy(log_mass, scratch.at[1], sems.at[1]),
        pltpu.make_async_copy(sources, sources_here, sems.at[2]),
        pltpu.make_async_copy(targets, targets_here, sems.at[3]),
    ]
    for copy in copies:
        copy.start()
    copies[0].wait()
    copies[1].wait()
    bias[...] = scratch[0] + EPSILON * scratch[1]
    copies[2].wait()
    copies[3].wait()


def load(sources, targets, potentials, log_mass):
    rows = potentials.shape[0] // LANES
    return pl.pallas_call(
        load_kernel,
        out_shape=(
            pltpu.VMEM(sources.shape, sources.dtype),
            pltpu.VMEM(targets.shape, targets.dtype),
            pltpu.VMEM((rows, LANES), jnp.float32),
        ),
        in_specs=[ANY] * 4,
        out_specs=(VMEM,) * 3,
        scratch_shapes=[pltpu.VMEM((2, rows, LANES), jnp.float32), pltpu.SemaphoreType.DMA((4,))],
    )(sources, targets, potentials.reshape(rows, LANES), log_mass.reshape(rows, LANES))


def place_targets(tgt_own, tgt_far, bias_ref, lhs):
    count = tgt_own.shape[1]
    width = tgt_own.shape[0] + tgt_far.shape[0]
    step = min(1024, count)
    for start in range(0, count, step):
        cols = slice(start, start + step)
        points = jnp.concatenate([tgt_own[:, cols], tgt_far[:, cols]], axis=0)
        wide = points.astype(jnp.float32)
        half = 0.5 * jnp.sum(wide * wide, axis=0, keepdims=True)
        first, second, third = split3(bias_ref[:, cols] - half)
        place = lax.broadcasted_iota(jnp.int32, (LANES - width, step), 0)
        extra = jnp.where(place < 6, 1.0, 0.0)
        for k, part in enumerate((first, second, third)):
            extra = jnp.where(place == k, part, extra)
        lhs[cols, :] = jnp.concatenate([points, extra.astype(jnp.bfloat16)], axis=0).T


def place_sources(order, src_ref, rhs):
    width, rows = src_ref.shape
    points = src_ref[...].astype(jnp.float32)
    me = lax.axis_index("src")
    n_src = len(order)
    part = width // n_src
    blocks = [points[k * part : (k + 1) * part] for k in range(n_src)]
    for bit in range(n_src.bit_length() - 1):
        turned = ((me >> bit) & 1) == 1
        blocks = [jnp.where(turned, blocks[k ^ (1 << bit)], blocks[k]) for k in range(n_src)]
    points = jnp.concatenate([blocks[k] for k in order], axis=0)
    rhs[:width, :] = points.astype(jnp.bfloat16)
    place = lax.broadcasted_iota(jnp.int32, (LANES - width, rows), 0)
    rhs[width:, :] = jnp.where(place < 3, 1.0, 0.0).astype(jnp.bfloat16)


def sources_kernel(order, *refs):
    count = len(refs) // 2
    for src_ref, rhs in zip(refs[:count], refs[count:], strict=True):
        place_sources(order, src_ref, rhs)


def placed_sources(order, held):
    return pl.pallas_call(
        functools.partial(sources_kernel, order),
        out_shape=tuple(pltpu.VMEM((LANES, piece.shape[1]), jnp.bfloat16) for piece in held),
        in_specs=[VMEM] * len(held),
        out_specs=(VMEM,) * len(held),
        cost_estimate=pl.CostEstimate(flops=1 << 30, bytes_accessed=0, transcendentals=0),
        compiler_params=pltpu.CompilerParams(vmem_limit_bytes=8 << 20),
    )(*held)


def log_sums(width, lhs, rhs, out_ref):
    count, rows = lhs.shape[0], rhs.shape[1]

    def product(j, block):
        chunk = pl.ds(pl.multiple_of(j * CHUNK, CHUNK), CHUNK)
        found = jnp.dot(lhs[chunk, :], block, preferred_element_type=jnp.float32)
        return found.reshape(CHUNK // 8, 8, found.shape[1])

    place = lax.broadcasted_iota(jnp.int32, (LANES - width, WIDE), 0)
    for start in range(0, rows, WIDE):
        cols = slice(start, start + WIDE)
        high = jnp.max(jnp.max(product(0, rhs[:, cols]), axis=0), axis=0, keepdims=True)
        extra = jnp.where(place < 3, 1.0, 0.0)
        for k, part in enumerate(split3(-high)):
            extra = jnp.where(place == 3 + k, part, extra)
        rhs[width:, cols] = extra.astype(jnp.bfloat16)
        out_ref[:, cols] = high * RATE
    worst = jnp.zeros((1, WIDE), jnp.float32)
    for start in range(0, rows, WIDE):
        cols = slice(start, start + WIDE)
        block = rhs[:, cols]
        total = jnp.zeros((8, WIDE), jnp.float32)
        for j in range(count // CHUNK):
            total = total + jnp.sum(jnp.exp2(product(j, block) * RATE), axis=0)
        row_sum = jnp.sum(total, axis=0, keepdims=True)
        out_ref[:, cols] += jnp.log2(row_sum)
        worst = jnp.maximum(worst, row_sum)

    @pl.when(jnp.logical_not(jnp.max(worst) < jnp.inf))
    def _():
        for start in range(0, rows, WIDE):
            cols = slice(start, start + WIDE)
            extra = jnp.where(place < 3, 1.0, 0.0)
            rhs[width:, cols] = extra.astype(jnp.bfloat16)
            block = rhs[:, cols]

            def step(j, carry):
                top, total = carry
                scores = product(j, block) * RATE
                higher = jnp.maximum(top, jnp.max(scores, axis=0))
                total = total * jnp.exp2(top - higher) + jnp.sum(jnp.exp2(scores - higher[None]), axis=0)
                return higher, total

            first = jnp.max(product(0, block) * RATE, axis=0)
            top, total = lax.fori_loop(0, count // CHUNK, step, (first, jnp.zeros_like(first)))
            row_top = jnp.max(top, axis=0, keepdims=True)
            row_sum = jnp.sum(total * jnp.exp2(top - row_top), axis=0, keepdims=True)
            out_ref[:, cols] = row_top + jnp.log2(row_sum)


def first_kernel(placed, tgt_own, tgt_far, bias_ref, out_ref, lhs, rhs):
    place_targets(tgt_own, tgt_far, bias_ref, lhs)
    rhs[...] = placed[...]
    log_sums(tgt_own.shape[0] + tgt_far.shape[0], lhs, rhs, out_ref)


def next_kernel(width, placed, lhs, out_ref, rhs):
    rhs[...] = placed[...]
    log_sums(width, lhs, rhs, out_ref)


def estimate(rows, count):
    return pl.CostEstimate(flops=2 * rows * count * LANES, bytes_accessed=2 * count * LANES, transcendentals=rows * count)


def first_logs(placed, tgt_own, tgt_far, bias):
    count, rows = tgt_own.shape[1], placed.shape[1]
    return pl.pallas_call(
        first_kernel,
        out_shape=(pltpu.VMEM((1, rows), jnp.float32), pltpu.VMEM((count, LANES), jnp.bfloat16)),
        in_specs=[VMEM] * 4,
        out_specs=(VMEM, VMEM),
        scratch_shapes=[pltpu.VMEM((LANES, rows), jnp.bfloat16)],
        cost_estimate=estimate(rows, count),
        compiler_params=pltpu.CompilerParams(vmem_limit_bytes=48 << 20),
    )(placed, tgt_own, tgt_far, bias)


def next_logs(width, placed, lhs):
    count, rows = lhs.shape[0], placed.shape[1]
    return pl.pallas_call(
        functools.partial(next_kernel, width),
        out_shape=pltpu.VMEM((1, rows), jnp.float32),
        in_specs=[VMEM] * 2,
        out_specs=VMEM,
        scratch_shapes=[pltpu.VMEM((LANES, rows), jnp.bfloat16)],
        cost_estimate=estimate(rows, count),
        compiler_params=pltpu.CompilerParams(vmem_limit_bytes=48 << 20),
    )(placed, lhs)


def join(left, right):
    top = jnp.maximum(left, right)
    return top + jnp.log2(1.0 + jnp.exp2(-jnp.abs(left - right)))


def gather(value, masks, axis):
    for mask in masks:
        value = jnp.concatenate([value, flip(value, mask)], axis=axis)
    return value


def on_device(sources, targets, potentials, log_mass):
    n_src, n_tgt = lax.axis_size("src"), lax.axis_size("tgt")
    src_bits, tgt_bits = n_src.bit_length() - 1, n_tgt.bit_length() - 1
    shared = min(2, tgt_bits)
    masks = [(1 << bit) | n_tgt for bit in range(shared - 1, -1, -1)]
    col_masks = [1 << bit for bit in range(tgt_bits - 1, shared - 1, -1)]
    row_masks = [n_tgt << bit for bit in range(1, src_bits)]

    sources_here, targets_here, bias = load(sources, targets, potentials, log_mass)
    held = [sources]
    for mask in masks:
        whole = sources if len(held) == 1 else jnp.concatenate([sources_here, *held[1:]], axis=1)
        held.append(flip(whole, mask))
    held[0] = sources_here
    if len(col_masks) == 1 and len(row_masks) == 1:
        beside = flip(targets, col_masks[0])
        below = flip(targets, row_masks[0])
        corner = flip(beside, row_masks[0])
        bias, _ = lax.optimization_barrier((bias, held[1]))
        there = flip(bias, col_masks[0])
        there, held[-1] = lax.optimization_barrier((there, held[-1]))
        bias = jnp.concatenate([bias, there], axis=0)
        upper = jnp.concatenate([targets_here, beside], axis=1)
        lower = jnp.concatenate([below, corner], axis=1)
        own = jnp.concatenate([upper, lower], axis=0)
    else:
        own = gather(gather(targets_here, col_masks, 1), row_masks, 0)
        bias = gather(bias, col_masks, 0)
    bias = bias.reshape(1, -1)
    far = flip(own, n_tgt)
    order = (*range(0, n_src, 2), *range(1, n_src, 2))
    placed = placed_sources(order, held)

    owned = sources.shape[1]
    arrived = []
    logs, lhs = first_logs(placed[-1], own, far, bias)
    for k in range(shared, 0, -1):
        for other in arrived:
            logs = join(logs, other[:, owned << (k - 1) : owned << k])
        arrived.append(flip(logs, masks[k - 1]))
        logs = next_logs(sources.shape[0], placed[k - 1], lhs)
    parts = [logs, *(other[:, :owned] for other in arrived)]
    top = functools.reduce(jnp.maximum, parts)
    logs = top + jnp.log2(sum(jnp.exp2(part - top) for part in parts))
    wide = sources.astype(jnp.float32)
    return 0.5 * jnp.sum(wide * wide, axis=0) - (1.0 / RATE) * logs[0]


def solution(mesh):
    in_specs = (P(None, ("src", "tgt")), P("src", "tgt"), P("tgt"), P("tgt"))
    out_specs = P(("src", "tgt"))
    return jax.shard_map(
        on_device, mesh=mesh, in_specs=in_specs, out_specs=out_specs, check_vma=False
    )
```
